32 devices in a mesh: row: 8 (over y, x, core), col: 4 (over z).
Axes of the slice: x: 2, y: 2, z: 4, core: 2. Of those that a mesh axis runs over, the one named last changes fastest.
Arguments:
- pair_rep: bfloat16 [512, 512, 128], P('row', 'col'), may hold values from -6 to 6
- token_mask: int32 [512], replicated, may hold values from 0 to 1, as said below
- in_gain: float32 [128], replicated, may hold values from 0.5 to 2
- in_bias: float32 [128], replicated, may hold values from -3 to 3
- left_weight: bfloat16 [128, 256], replicated, may hold values from -0.5 to 0.5
- right_weight: bfloat16 [128, 256], replicated, may hold values from -0.5 to 0.5
- gate_weight: bfloat16 [128, 128], replicated, may hold values from -0.5 to 0.5
- out_gain: float32 [128], replicated, may hold values from 0.5 to 2
- out_bias: float32 [128], replicated, may hold values from -3 to 3
- out_weight: bfloat16 [128, 128], replicated, may hold values from -0.5 to 0.5
Outputs:
- update: bfloat16 [512, 512, 128], P('row', 'col')
The draws below stay inside these ranges and needn't reach their ends.
Inputs may be any that keep to these rules, and one draw needn't show every extreme that they name: `token_mask`: tokens lie in chains of 64 consecutive slots; in each chain a leading run of 32 to 64 slots is 1 and the rest is 0; the first chain is full and the second holds exactly 32 real tokens.
All inputs are finite; a program needn't handle non-finite values.
Results may differ from the reference program's by a relative error of at most 0.0053.
Values may be sent and summed in bfloat16 or wider, within the bound.
No kernel may reach another device: no remote copies, remote signals or barrier semaphores. Data moves between devices by JAX's collectives and lax.ppermute only.
A program may use at most 128 MiB of HBM per device.

```python
import math
import jax
import jax.numpy as jnp
from jax import lax

PAIR = 128
HID = 128
CHAIN = 64
TOKENS = 512


def draw_token_mask(key, part):
    chains = TOKENS // CHAIN
    lengths = jax.random.randint(key, (chains,), CHAIN // 2, CHAIN + 1).astype(jnp.int32)
    lengths = lengths.at[0].set(CHAIN).at[1].set(CHAIN // 2)
    slots = jnp.arange(TOKENS, dtype=jnp.int32)
    owner = slots // CHAIN
    return (slots % CHAIN < lengths[owner]).astype(jnp.int32)


def levels(stream_key, shape, pieces, low, top_value):
    def one(dim, blocks):
        heights = jax.random.uniform(jax.random.fold_in(jax.random.fold_in(stream_key, 6), dim), (blocks,), jnp.float32, low / len(pieces), top_value / len(pieces))
        return jnp.repeat(jnp.exp(heights), shape[dim] // blocks).reshape((-1,) + (1,) * (len(shape) - dim - 1))

    gain = one(*pieces[0])
    for cut in pieces[1:]:
        gain = gain * one(*cut)
    return gain


def scatter_about(key, dims, scale, limit, cuts=(), kind=jnp.bfloat16):
    values = scale * jax.random.normal(key, dims, jnp.float32)
    if cuts:
        values = values * levels(key, dims, cuts, -0.22, 0.18)
    return jnp.clip(values, -limit, limit).astype(kind)


def setup_inputs(seed: int = 0) -> dict:
    key_list = jax.random.split(jax.random.key(seed), 11)
    pair_rep = scatter_about(key_list[0], (TOKENS, TOKENS, PAIR), 1.0, 6.0, ((0, 8), (1, 4)))
    token_mask = draw_token_mask(jax.random.fold_in(key_list[10], 71), 0)
    in_gain = jnp.clip(jnp.exp(jax.random.uniform(key_list[2], (PAIR,), jnp.float32, math.log(0.5), math.log(2.0))), 0.5, 2.0)
    in_bias = scatter_about(key_list[3], (PAIR,), 0.5, 3.0, (), jnp.float32)
    left_weight = scatter_about(key_list[4], (PAIR, 2 * HID), PAIR ** -0.5, 0.5)
    right_weight = scatter_about(key_list[5], (PAIR, 2 * HID), PAIR ** -0.5, 0.5)
    gate_weight = scatter_about(key_list[6], (PAIR, PAIR), PAIR ** -0.5, 0.5)
    out_gain = jnp.clip(jnp.exp(jax.random.uniform(key_list[7], (HID,), jnp.float32, math.log(0.5), math.log(2.0))), 0.5, 2.0)
    out_bias = scatter_about(key_list[8], (HID,), 0.5, 3.0, (), jnp.float32)
    out_weight = scatter_about(key_list[9], (HID, PAIR), HID ** -0.5, 0.5)
    return dict(pair_rep=pair_rep, token_mask=token_mask, in_gain=in_gain, in_bias=in_bias, left_weight=left_weight, right_weight=right_weight, gate_weight=gate_weight, out_gain=out_gain, out_bias=out_bias, out_weight=out_weight)


EPS = 1e-05

def layer_norm(values, gain_vec, bias_vec):
    average = lax.optimization_barrier(jnp.mean(values, axis=-1, keepdims=True))
    centered = values - average
    variance = lax.optimization_barrier(jnp.mean(centered * centered, axis=-1, keepdims=True))
    return centered * lax.rsqrt(variance + EPS) * gain_vec + bias_vec

def edge_values(normed, weight, pair_mask):
    projected = jnp.dot(normed, weight, preferred_element_type=jnp.float32)
    return (jax.nn.sigmoid(projected[:, :HID]) * projected[:, HID:] * pair_mask).astype(jnp.bfloat16)

def reference(pair_rep, token_mask, in_gain, in_bias, left_weight, right_weight, gate_weight, out_gain, out_bias, out_weight):
    flat_pair = pair_rep.reshape(TOKENS * TOKENS, PAIR).astype(jnp.float32)
    normed = layer_norm(flat_pair, in_gain, in_bias).astype(jnp.bfloat16)
    validity = token_mask.astype(jnp.float32)
    pair_mask = (validity[:, None] * validity[None, :]).reshape(TOKENS * TOKENS, 1)
    left_value = edge_values(normed, left_weight, pair_mask)
    right_value = edge_values(normed, right_weight, pair_mask)
    gate_value = jax.nn.sigmoid(jnp.dot(normed, gate_weight, preferred_element_type=jnp.float32))
    left_first = left_value.reshape(TOKENS, TOKENS, HID).transpose(2, 0, 1).astype(jnp.float32)
    right_first = right_value.reshape(TOKENS, TOKENS, HID).transpose(2, 0, 1).astype(jnp.float32)
    product = jnp.einsum('hik,hjk->hij', left_first, right_first, precision=lax.Precision.HIGHEST)
    product = product.transpose(1, 2, 0).reshape(TOKENS * TOKENS, HID)
    final_norm = layer_norm(product, out_gain, out_bias).astype(jnp.bfloat16)
    update = gate_value * jnp.dot(final_norm, out_weight, preferred_element_type=jnp.float32)
    return update.reshape(TOKENS, TOKENS, PAIR).astype(jnp.bfloat16)
```

```python
import functools

import jax
import jax.numpy as jnp
from jax import lax
from jax.experimental import pallas as pl
from jax.experimental.pallas import tpu as pltpu
from jax.sharding import PartitionSpec as P

EPS = 1e-05
F32 = jnp.float32
BF16 = jnp.bfloat16
ROW_TILE = 16
PARAMS = pltpu.CompilerParams(vmem_limit_bytes=56 * 2**20)


def whole(array):
    return pl.BlockSpec(array.shape, lambda *_: (0,) * array.ndim)


def project(normed, mask_ref, left_ref, right_ref, out_ref, low, width):
    rows, cols, pair_width = normed.shape
    hidden = left_ref.shape[1] // 2
    half = jnp.asarray(0.5, BF16)
    left = left_ref[...].T * half
    right = right_ref[...].T * half
    weight = jnp.concatenate(
        [
            left[low : low + width],
            right[low : low + width],
            left[hidden + low : hidden + low + width],
            right[hidden + low : hidden + low + width],
        ],
        0,
    )
    pieces = []
    for i in range(0, rows, 2):
        two = normed[i : i + 2].reshape(2 * cols, pair_width)
        proj = lax.dot_general(
            weight, two, (((1,), (1,)), ((), ())), preferred_element_type=F32
        )
        value = ((jnp.tanh(proj[: 2 * width]) + 1.0) * proj[2 * width :]).astype(BF16)
        pieces += [value[:, :cols], value[:, cols:]]
    value = jnp.swapaxes(jnp.stack(pieces, 0), 0, 1) * mask_ref[...][None]
    dests, _, share = out_ref.shape[:3]
    for side in range(2):
        part = value[side * width : (side + 1) * width]
        out_ref[:, side] = part.reshape(dests, share, rows, cols)


def first_kernel(
    pair_ref, mask_ref, left_ref, right_ref, gain_ref, bias_ref, normed_ref, out_ref, *, low, width
):
    value = pair_ref[...].astype(F32)
    average = jnp.mean(value, axis=-1, keepdims=True)
    centered = value - average
    variance = jnp.mean(centered * centered, axis=-1, keepdims=True)
    normed = (centered * lax.rsqrt(variance + EPS) * gain_ref[...] + bias_ref[...]).astype(BF16)
    normed_ref[...] = normed
    project(normed, mask_ref, left_ref, right_ref, out_ref, low, width)


def later_kernel(normed_ref, mask_ref, left_ref, right_ref, out_ref, *, low, width):
    project(normed_ref[...], mask_ref, left_ref, right_ref, out_ref, low, width)


def gate_kernel(normed_ref, weight_ref, gate_ref):
    rows, cols, pair_width = normed_ref.shape
    half = jnp.asarray(0.5, BF16)
    proj = jnp.dot(
        normed_ref[...].reshape(rows * cols, pair_width),
        weight_ref[...] * half,
        preferred_element_type=F32,
    )
    gate_ref[...] = (0.5 * jnp.tanh(proj) + 0.5).reshape(gate_ref.shape)


def panel(ref, side, start, count):
    parts = []
    for z in range(ref.shape[1]):
        block = ref[pl.ds(start, count), z, side, 0]
        parts.append(block.reshape(count * block.shape[1], block.shape[2]))
    return jnp.concatenate(parts, 1)


def times(left, right):
    return lax.dot_general(left, right, (((1,), (1,)), ((), ())), preferred_element_type=F32)


def far_kernel(half_ref, edges_ref, far_ref):
    devices = edges_ref.shape[0]
    left = panel(edges_ref, 0, 0, devices)
    right = panel(edges_ref, 1, (1 - half_ref[0]) * (devices // 2), devices // 2)
    far_ref[0] = times(left, right).astype(BF16)


def near_kernel(half_ref, edges_ref, far_ref, out_ref):
    devices, groups, _, rows, cols = out_ref.shape
    left = panel(edges_ref, 0, 0, devices)
    right = panel(edges_ref, 1, half_ref[0] * (devices // 2), devices // 2)
    total = (times(left, right) + far_ref[0].astype(F32)).astype(BF16)
    for z in range(groups):
        out_ref[:, z, 0] = total[:, z * cols : (z + 1) * cols].reshape(devices, rows, cols)


def last_kernel(*refs):
    gate_ref, gain_ref, bias_ref, weight_ref = refs[:4]
    out_ref = refs[-1]
    rows, cols = gate_ref.shape[:2]
    parts = []
    for ref in refs[4:-1]:
        parts.append(ref[...].reshape(ref.shape[0] * ref.shape[1], rows, cols))
    value = jnp.swapaxes(jnp.concatenate(parts, 0), 0, 1)
    weight = weight_ref[...]
    for i in range(rows):
        product = value[i].astype(F32)
        average = jnp.mean(product, axis=0, keepdims=True)
        centered = product - average
        variance = jnp.mean(centered * centered, axis=0, keepdims=True)
        normed = centered * lax.rsqrt(variance + EPS) * gain_ref[...] + bias_ref[...]
        update = lax.dot_general(
            normed.astype(BF16), weight, (((0,), (0,)), ((), ())), preferred_element_type=F32
        )
        out_ref[i] = (gate_ref[i] * update).astype(BF16)


def shards(
    pair_rep,
    token_mask,
    in_gain,
    in_bias,
    left_weight,
    right_weight,
    gate_weight,
    out_gain,
    out_bias,
    out_weight,
):
    rows, cols, pair_width = pair_rep.shape
    hidden = out_weight.shape[0]
    row_count = lax.axis_size("row")
    col_count = lax.axis_size("col")
    group_cols = col_count // 2
    half = lax.axis_index("col") // group_cols
    members = row_count * group_cols
    share = hidden // members
    chunks = 2 if share % 2 == 0 else 1
    share //= chunks
    width = hidden // chunks
    axes = ("row", "col")
    groups = [
        [r * col_count + h * group_cols + z for r in range(row_count) for z in range(group_cols)]
        for h in range(2)
    ]
    across = [(c, (c + group_cols) % col_count) for c in range(col_count)]
    half_arg = jnp.reshape(half, (1,)).astype(jnp.int32)

    row_valid = lax.dynamic_slice_in_dim(token_mask, lax.axis_index("row") * rows, rows)
    col_valid = lax.dynamic_slice_in_dim(token_mask, lax.axis_index("col") * cols, cols)
    mask = (row_valid[:, None] * col_valid[None, :]).astype(BF16)

    tile = min(ROW_TILE, rows)
    steps = rows // tile
    by_row = lambda *tail: pl.BlockSpec((tile,) + tail, lambda i: (i,) + (0,) * len(tail))
    edge_shape = jax.ShapeDtypeStruct((members, 2, share, rows, cols), BF16)
    edge_spec = pl.BlockSpec((members, 2, share, tile, cols), lambda i: (0, 0, 0, i, 0))
    edges = []
    normed, first = pl.pallas_call(
        functools.partial(first_kernel, low=0, width=width),
        grid=(steps,),
        in_specs=[
            by_row(cols, pair_width),
            by_row(cols),
            whole(left_weight),
            whole(right_weight),
            whole(in_gain[None]),
            whole(in_bias[None]),
        ],
        out_specs=[by_row(cols, pair_width), edge_spec],
        out_shape=[jax.ShapeDtypeStruct(pair_rep.shape, BF16), edge_shape],
        compiler_params=PARAMS,
        name="norm_project",
    )(pair_rep, mask, left_weight, right_weight, in_gain[None], in_bias[None])
    edges.append(first)
    for t in range(1, chunks):
        edges.append(
            pl.pallas_call(
                functools.partial(later_kernel, low=t * width, width=width),
                grid=(steps,),
                in_specs=[
                    by_row(cols, pair_width),
                    by_row(cols),
                    whole(left_weight),
                    whole(right_weight),
                ],
                out_specs=edge_spec,
                out_shape=edge_shape,
                compiler_params=PARAMS,
                cost_estimate=pl.CostEstimate(
                    flops=4 * rows * cols * pair_width * width * 2,
                    bytes_accessed=3 * rows * cols * pair_width * 2,
                    transcendentals=rows * cols * width * 2,
                ),
                name="project",
            )(normed, mask, left_weight, right_weight)
        )
    gate = pl.pallas_call(
        gate_kernel,
        grid=(steps,),
        in_specs=[by_row(cols, pair_width), whole(gate_weight)],
        out_specs=by_row(cols, pair_width),
        out_shape=jax.ShapeDtypeStruct(pair_rep.shape, F32),
        compiler_params=PARAMS,
        cost_estimate=pl.CostEstimate(
            flops=2 * rows * cols * pair_width * pair_width,
            bytes_accessed=rows * cols * pair_width * 6,
            transcendentals=rows * cols * pair_width,
        ),
        name="gate",
    )(normed, gate_weight)

    def exchange(value):
        return lax.all_to_all(value, axes, 0, 0, axis_index_groups=groups, tiled=True)

    tokens = row_count * rows
    near_tokens = group_cols * cols
    one_h = pl.BlockSpec(
        (row_count, group_cols, 2, 1, rows, cols), lambda h, _: (0, 0, 0, h, 0, 0)
    )
    far_spec = pl.BlockSpec((1, tokens, near_tokens), lambda h, _: (h, 0, 0))
    product_cost = pl.CostEstimate(
        flops=2 * share * tokens * near_tokens * near_tokens,
        bytes_accessed=share * tokens * near_tokens * 6,
        transcendentals=0,
    )
    arrived = []
    fars = []
    for t in range(chunks):
        here = exchange(edges[t]).reshape(row_count, group_cols, 2, share, rows, cols)
        arrived.append(here)
        far = pl.pallas_call(
            far_kernel,
            grid_spec=pltpu.PrefetchScalarGridSpec(
                num_scalar_prefetch=1, grid=(share,), in_specs=[one_h], out_specs=far_spec
            ),
            out_shape=jax.ShapeDtypeStruct((share, tokens, near_tokens), BF16),
            compiler_params=PARAMS,
            cost_estimate=product_cost,
            name="far_product",
        )(half_arg, here)
        fars.append(lax.ppermute(far, "col", across))
    back = []
    for t in range(chunks):
        total = pl.pallas_call(
            near_kernel,
            grid_spec=pltpu.PrefetchScalarGridSpec(
                num_scalar_prefetch=1,
                grid=(share,),
                in_specs=[one_h, far_spec],
                out_specs=pl.BlockSpec(
                    (row_count, group_cols, 1, rows, cols), lambda h, _: (0, 0, h, 0, 0)
                ),
            ),
            out_shape=jax.ShapeDtypeStruct((row_count, group_cols, share, rows, cols), BF16),
            compiler_params=PARAMS,
            cost_estimate=product_cost,
            name="near_product",
        )(half_arg, arrived[t], fars[t])
        back.append(exchange(total.reshape(members, share, rows, cols)))

    gain_cols = jnp.broadcast_to(out_gain[:, None], (hidden, cols))
    bias_cols = jnp.broadcast_to(out_bias[:, None], (hidden, cols))
    piece = pl.BlockSpec((members, share, tile, cols), lambda i: (0, 0, i, 0))
    return pl.pallas_call(
        last_kernel,
        grid=(steps,),
        in_specs=[
            by_row(cols, pair_width),
            whole(gain_cols),
            whole(bias_cols),
            whole(out_weight),
        ]
        + [piece] * chunks,
        out_specs=by_row(cols, pair_width),
        out_shape=jax.ShapeDtypeStruct(pair_rep.shape, BF16),
        compiler_params=PARAMS,
        name="norm_out",
    )(gate, gain_cols, bias_cols, out_weight, *back)


def solution(mesh):
    placed = (P("row", "col", None), P(), P(), P(), P(), P(), P(), P(), P(), P())
    return jax.shard_map(
        shards, mesh=mesh, in_specs=placed, out_specs=P("row", "col", None), check_vma=False
    )
```

```python
import functools

import jax
import jax.numpy as jnp
from jax import lax
from jax.experimental import pallas as pl
from jax.experimental.pallas import tpu as pltpu
from jax.sharding import PartitionSpec as P

EPS = 1e-05
F32 = jnp.float32
BF16 = jnp.bfloat16
ROW_TILE = 16
CHUNKS = 2
PARAMS = pltpu.CompilerParams(vmem_limit_bytes=56 * 2**20)
NT = (((1,), (1,)), ((), ()))
SIZES = ((12, 0), (13, 2), (14, 4), (16, 16))


def whole(array):
    return pl.BlockSpec(array.shape, lambda *_: (0,) * array.ndim)


def dot(left, right, dims=(((1,), (0,)), ((), ()))):
    return lax.dot_general(left, right, dims, preferred_element_type=F32)


def project(normed, step, tokens_ref, cols_ref, left_ref, right_ref, out_ref, low, width):
    rows, cols, pair_width = normed.shape
    hidden = left_ref.shape[1] // 2
    half = jnp.asarray(0.5, BF16)
    left = left_ref[...].T * half
    right = right_ref[...].T * half
    weight = jnp.concatenate(
        [
            left[low : low + width],
            right[low : low + width],
            left[hidden + low : hidden + low + width],
            right[hidden + low : hidden + low + width],
        ],
        0,
    )
    start = (lax.axis_index("row") * pl.num_programs(0) + step) * rows
    col_valid = cols_ref[lax.axis_index("col")].astype(F32)
    pieces = []
    for i in range(0, rows, 2):
        two = normed[i : i + 2].reshape(2 * cols, pair_width)
        proj = dot(weight, two, NT)
        valid = jnp.concatenate(
            [col_valid * tokens_ref[start + i + n].astype(F32) for n in range(2)], 1
        )
        value = (jnp.tanh(proj[: 2 * width]) + 1.0) * (proj[2 * width :] * valid)
        value = value.astype(BF16)
        pieces += [value[:, :cols], value[:, cols:]]
    value = jnp.swapaxes(jnp.stack(pieces, 0), 0, 1)
    dests, _, share = out_ref.shape[:3]
    for side in range(2):
        part = value[side * width : (side + 1) * width]
        out_ref[:, side] = part.reshape(dests, share, rows, cols)


def first_kernel(
    tokens_ref, cols_ref, pair_ref, left_ref, right_ref, gain_ref, bias_ref, normed_ref, out_ref, *, width
):
    value = pair_ref[...].astype(F32)
    average = jnp.mean(value, axis=-1, keepdims=True)
    centered = value - average
    variance = jnp.mean(centered * centered, axis=-1, keepdims=True)
    normed = (centered * lax.rsqrt(variance + EPS) * gain_ref[...] + bias_ref[...]).astype(BF16)
    normed_ref[...] = normed
    project(normed, pl.program_id(0), tokens_ref, cols_ref, left_ref, right_ref, out_ref, 0, width)


def later_kernel(tokens_ref, cols_ref, normed_ref, left_ref, right_ref, out_ref, *, low, width):
    step = pl.program_id(0)
    project(normed_ref[...], step, tokens_ref, cols_ref, left_ref, right_ref, out_ref, low, width)


def gate_kernel(normed_ref, weight_ref, gate_ref):
    rows, cols, pair_width = normed_ref.shape
    half = jnp.asarray(0.5, BF16)
    proj = dot(normed_ref[...].reshape(rows * cols, pair_width), weight_ref[...] * half)
    gate_ref[...] = (0.5 * jnp.tanh(proj) + 0.5).reshape(gate_ref.shape)


def pick(valid, count):
    size = valid.shape[1]
    above = lax.broadcasted_iota(jnp.int32, (size, size), 0)
    below = lax.broadcasted_iota(jnp.int32, (size, size), 1)
    through = dot(valid, jnp.where(above <= below, 1.0, 0.0).astype(BF16))
    place = jnp.where(valid.astype(F32) > 0.5, through - 1.0, -1.0)[:1]
    order = lax.broadcasted_iota(jnp.int32, (count, size), 0).astype(F32)
    return jnp.where(order == place, 1.0, 0.0)


def picks_kernel(tokens_ref, all_ref, spread_ref, far_ref, near_ref):
    valid = jnp.broadcast_to(tokens_ref[...].astype(F32), (16, tokens_ref.shape[1])).astype(BF16)
    chosen = pick(valid, all_ref.shape[0])
    all_ref[...] = chosen.astype(BF16)
    spread_ref[...] = chosen.T.astype(BF16)
    size = far_ref.shape[1]
    low = pick(valid[:, :size], far_ref.shape[0]).astype(BF16)
    high = pick(valid[:, size:], far_ref.shape[0]).astype(BF16)
    second = lax.axis_index("col") // (lax.axis_size("col") // 2) == 1
    far_ref[...] = jnp.where(second, low, high)
    near_ref[...] = jnp.where(second, high, low)


def panel(ref, side, start, count):
    parts = []
    for z in range(ref.shape[1]):
        block = ref[pl.ds(start, count), z, side, 0]
        parts.append(block.reshape(count * block.shape[1], block.shape[2]))
    return jnp.concatenate(parts, 1)


def own_half():
    return lax.axis_index("col") // (lax.axis_size("col") // 2)


def far_kernel(all_ref, pick_ref, edges_ref, far_ref):
    devices = edges_ref.shape[0]
    left = panel(edges_ref, 0, 0, devices)
    right = panel(edges_ref, 1, (1 - own_half()) * (devices // 2), devices // 2)
    count, size = pick_ref.shape
    main = left.shape[0] * 3 // 4
    left = dot(all_ref[...], left).astype(BF16)
    few = dot(pick_ref[...], right).astype(BF16)
    part = dot(few, left[:main], NT).astype(BF16)
    at = 0
    for n in range(0, main, 128):
        far_ref[0, at : at + count] = part[:, n : n + 128]
        at += count
    rest = left.shape[0] - main
    if rest:
        part = dot(left[main:], right, NT).astype(BF16)
        for n in range(0, size, 128):
            far_ref[0, at : at + rest] = part[:, n : n + 128]
            at += rest


def near_kernel(spread_ref, pick_ref, edges_ref, far_ref, out_ref):
    devices, groups, _, rows, cols = out_ref.shape
    left = panel(edges_ref, 0, 0, devices)
    right = panel(edges_ref, 1, own_half() * (devices // 2), devices // 2)
    total = dot(left, right, NT)
    count, size = pick_ref.shape
    main = left.shape[0] * 3 // 4
    at = main // 128 * count
    part = jnp.concatenate([far_ref[0, n : n + count] for n in range(0, at, count)], 1)
    part = dot(spread_ref[:, :main], part, NT).astype(BF16)
    total = total + dot(part, pick_ref[...])
    rest = spread_ref.shape[1] - main
    if rest:
        ends = range(at, at + size // 128 * rest, rest)
        part = jnp.concatenate([far_ref[0, n : n + rest] for n in ends], 1)
        total = total + dot(spread_ref[:, main:], part)
    total = total.astype(BF16)
    for z in range(groups):
        out_ref[:, z, 0] = total[:, z * cols : (z + 1) * cols].reshape(devices, rows, cols)


def last_kernel(*refs):
    gate_ref, gain_ref, bias_ref, weight_ref = refs[:4]
    out_ref = refs[-1]
    rows, cols = gate_ref.shape[:2]
    hidden = weight_ref.shape[0]
    parts = []
    for ref in refs[4:-1]:
        parts.append(ref[...].reshape(ref.shape[0] * ref.shape[1], rows, cols))
    value = jnp.swapaxes(jnp.concatenate(parts, 0), 0, 1)
    weight = weight_ref[...]
    gain = jnp.broadcast_to(gain_ref[...], (cols, hidden)).T
    bias = jnp.broadcast_to(bias_ref[...], (cols, hidden)).T
    for i in range(rows):
        product = value[i].astype(F32)
        average = jnp.mean(product, axis=0, keepdims=True)
        centered = product - average
        variance = jnp.mean(centered * centered, axis=0, keepdims=True)
        normed = centered * lax.rsqrt(variance + EPS) * gain + bias
        update = dot(normed.astype(BF16), weight, (((0,), (0,)), ((), ())))
        out_ref[i] = (gate_ref[i] * update).astype(BF16)


def shards(
    pair_rep,
    token_mask,
    in_gain,
    in_bias,
    left_weight,
    right_weight,
    gate_weight,
    out_gain,
    out_bias,
    out_weight,
):
    rows, cols, pair_width = pair_rep.shape
    hidden = out_weight.shape[0]
    row_count = lax.axis_size("row")
    col_count = lax.axis_size("col")
    group_cols = col_count // 2
    members = row_count * group_cols
    share = hidden // members
    chunks = CHUNKS if share % CHUNKS == 0 else 1
    share //= chunks
    width = hidden // chunks
    tokens = row_count * rows
    near_tokens = group_cols * cols
    axes = ("row", "col")
    groups = [
        [r * col_count + h * group_cols + z for r in range(row_count) for z in range(group_cols)]
        for h in range(2)
    ]
    across = [(c, (c + group_cols) % col_count) for c in range(col_count)]

    tile = min(ROW_TILE, rows)
    steps = rows // tile
    by_row = lambda *tail: pl.BlockSpec((tile,) + tail, lambda i: (i,) + (0,) * len(tail))
    edge_shape = jax.ShapeDtypeStruct((members, 2, share, rows, cols), BF16)
    edge_spec = pl.BlockSpec((members, 2, share, tile, cols), lambda i: (0, 0, 0, i, 0))
    col_tokens = token_mask.reshape(col_count, 1, cols)
    mask_specs = [pl.BlockSpec(memory_space=pltpu.SMEM), whole(col_tokens)]
    weight_specs = [whole(left_weight), whole(right_weight)]
    edges = []
    normed, first = pl.pallas_call(
        functools.partial(first_kernel, width=width),
        grid=(steps,),
        in_specs=mask_specs
        + [by_row(cols, pair_width)]
        + weight_specs
        + [whole(in_gain[None]), whole(in_bias[None])],
        out_specs=[by_row(cols, pair_width), edge_spec],
        out_shape=[jax.ShapeDtypeStruct(pair_rep.shape, BF16), edge_shape],
        compiler_params=PARAMS,
        name="norm_project",
    )(token_mask, col_tokens, pair_rep, left_weight, right_weight, in_gain[None], in_bias[None])

    def after(value, others):
        return lax.optimization_barrier((value, *others))[0] if others else value

    def exchange(value):
        return lax.all_to_all(value, axes, 0, 0, axis_index_groups=groups, tiled=True)

    def rest_of(sizes, normed, first, token_mask, col_tokens):
        few = near_tokens * sizes[0] // 16
        main = tokens * 3 // 4
        rest = (tokens - main) * sizes[1] // 16
        length = main // 128 * few + near_tokens // 128 * rest
        all_pick, spread, far_pick, near_pick = pl.pallas_call(
            picks_kernel,
            out_shape=[
                jax.ShapeDtypeStruct((main + rest, tokens), BF16),
                jax.ShapeDtypeStruct((tokens, main + rest), BF16),
                jax.ShapeDtypeStruct((few, near_tokens), BF16),
                jax.ShapeDtypeStruct((few, near_tokens), BF16),
            ],
            compiler_params=PARAMS,
            cost_estimate=pl.CostEstimate(
                flops=64 * tokens * tokens, bytes_accessed=6 * tokens * tokens, transcendentals=0
            ),
            name="picks",
        )(token_mask[None])
        edges = [first]
        for t in range(1, chunks):
            edges.append(
                pl.pallas_call(
                    functools.partial(later_kernel, low=t * width, width=width),
                    grid=(steps,),
                    in_specs=mask_specs + [by_row(cols, pair_width)] + weight_specs,
                    out_specs=edge_spec,
                    out_shape=edge_shape,
                    compiler_params=PARAMS,
                    cost_estimate=pl.CostEstimate(
                        flops=4 * rows * cols * pair_width * width * 2,
                        bytes_accessed=3 * rows * cols * pair_width * 2,
                        transcendentals=rows * cols * width * 2,
                    ),
                    name="project",
                )(token_mask, col_tokens, normed, left_weight, right_weight)
            )
        gate = pl.pallas_call(
            gate_kernel,
            grid=(steps,),
            in_specs=[by_row(cols, pair_width), whole(gate_weight)],
            out_specs=by_row(cols, pair_width),
            out_shape=jax.ShapeDtypeStruct(pair_rep.shape, F32),
            compiler_params=PARAMS,
            cost_estimate=pl.CostEstimate(
                flops=2 * rows * cols * pair_width * pair_width,
                bytes_accessed=rows * cols * pair_width * 6,
                transcendentals=rows * cols * pair_width,
            ),
            name="gate",
        )(normed, gate_weight)

        one_h = pl.BlockSpec(
            (row_count, group_cols, 2, 1, rows, cols), lambda h: (0, 0, 0, h, 0, 0)
        )
        far_spec = pl.BlockSpec((1, length, 128), lambda h: (h, 0, 0))
        product_cost = pl.CostEstimate(
            flops=6 * share * tokens * near_tokens * near_tokens,
            bytes_accessed=share * tokens * near_tokens * 6,
            transcendentals=0,
        )
        arrived = []
        sent = []
        fars = []
        for t in range(chunks):
            edge = after(edges[t], arrived[-1:])
            here = exchange(edge).reshape(row_count, group_cols, 2, share, rows, cols)
            arrived.append(here)
            far = pl.pallas_call(
                far_kernel,
                grid=(share,),
                in_specs=[whole(all_pick), whole(far_pick), one_h],
                out_specs=far_spec,
                out_shape=jax.ShapeDtypeStruct((share, length, 128), BF16),
                compiler_params=PARAMS,
                cost_estimate=product_cost,
                name="far_product",
            )(all_pick, far_pick, here)
            sent.append(far)
            fars.append(lax.ppermute(far, "col", across))
        back = []
        totals = []
        for t in range(chunks):
            total = pl.pallas_call(
                near_kernel,
                grid=(share,),
                in_specs=[whole(spread), whole(near_pick), one_h, far_spec],
                out_specs=pl.BlockSpec(
                    (row_count, group_cols, 1, rows, cols), lambda h: (0, 0, h, 0, 0)
                ),
                out_shape=jax.ShapeDtypeStruct((row_count, group_cols, share, rows, cols), BF16),
                compiler_params=PARAMS,
                cost_estimate=product_cost,
                name="near_product",
            )(spread, near_pick, arrived[t], after(fars[t], sent[t + 1 : t + 2] + totals[-1:]))
            totals.append(total)
            back.append(exchange(total.reshape(members, share, rows, cols)))

        piece = pl.BlockSpec((members, share, tile, cols), lambda i: (0, 0, i, 0))
        return pl.pallas_call(
            last_kernel,
            grid=(steps,),
            in_specs=[
                by_row(cols, pair_width),
                whole(out_gain[None]),
                whole(out_bias[None]),
                whole(out_weight),
            ]
            + [piece] * chunks,
            out_specs=by_row(cols, pair_width),
            out_shape=jax.ShapeDtypeStruct(pair_rep.shape, BF16),
            compiler_params=PARAMS,
            name="norm_out",
        )(gate, out_gain[None], out_bias[None], out_weight, *back)

    count = jnp.sum(token_mask.reshape(2, near_tokens), axis=1)
    most, over = jnp.max(count), jnp.sum(count) - tokens * 3 // 4
    fits = [
        (most <= near_tokens * few // 16) & (over <= tokens // 4 * rest // 16)
        for few, rest in SIZES[:-1]
    ]
    number = len(SIZES) - 1
    for n in range(len(SIZES) - 2, -1, -1):
        number = jnp.where(fits[n], n, number)
    branches = [functools.partial(rest_of, sizes) for sizes in SIZES]
    return lax.switch(number, branches, normed, first, token_mask, col_tokens)


def solution(mesh):
    placed = (P("row", "col", None), P(), P(), P(), P(), P(), P(), P(), P(), P())
    return jax.shard_map(
        shards, mesh=mesh, in_specs=placed, out_specs=P("row", "col", None), check_vma=False
    )
```

```python
import functools

import jax
import jax.numpy as jnp
from jax import lax
from jax.experimental import pallas as pl
from jax.experimental.pallas import tpu as pltpu
from jax.sharding import PartitionSpec as P

EPS = 1e-05
F32 = jnp.float32
BF16 = jnp.bfloat16
ROW_TILE = 16
CHUNKS = 2
NEAR_FLOPS = 2 * 10**10
PARAMS = pltpu.CompilerParams(vmem_limit_bytes=56 * 2**20)
NT = (((1,), (1,)), ((), ()))
SIZES = ((12, 3, 0), (13, 3, 1), (14, 3, 1), (16, 4, 0))


def whole(array):
    return pl.BlockSpec(array.shape, lambda *_: (0,) * array.ndim)


def dot(left, right, dims=(((1,), (0,)), ((), ()))):
    return lax.dot_general(left, right, dims, preferred_element_type=F32)


def project(normed, step, tokens_ref, mask_ref, left_ref, right_ref, out_ref, low, width):
    rows, cols, pair_width = normed.shape
    hidden = left_ref.shape[1] // 2
    half = jnp.asarray(0.5, BF16)
    left = left_ref[...].T * half
    right = right_ref[...].T * half
    weight = jnp.concatenate(
        [
            left[low : low + width],
            right[low : low + width],
            left[hidden + low : hidden + low + width],
            right[hidden + low : hidden + low + width],
        ],
        0,
    )
    start = (lax.axis_index("row") * pl.num_programs(0) + step) * rows
    tokens = mask_ref.shape[1]
    valid = jnp.broadcast_to(mask_ref[...], (8, tokens)).astype(F32)
    valid = pltpu.roll(valid, lax.rem(tokens - lax.axis_index("col") * cols, tokens), 1)
    valid = valid[:1, :cols]
    pieces = []
    for i in range(0, rows, 2):
        two = normed[i : i + 2].reshape(2 * cols, pair_width)
        proj = dot(weight, two, NT)
        pair_valid = jnp.concatenate(
            [valid * tokens_ref[start + i + n].astype(F32) for n in range(2)], 1
        )
        value = (jnp.tanh(proj[: 2 * width]) + 1.0) * (proj[2 * width :] * pair_valid)
        value = value.astype(BF16)
        pieces += [value[:, :cols], value[:, cols:]]
    value = jnp.swapaxes(jnp.stack(pieces, 0), 0, 1)
    dests, _, share = out_ref.shape[:3]
    for side in range(2):
        part = value[side * width : (side + 1) * width]
        out_ref[:, side] = part.reshape(dests, share, rows, cols)


def first_kernel(
    tokens_ref,
    mask_ref,
    pair_ref,
    left_ref,
    right_ref,
    gain_ref,
    bias_ref,
    normed_ref,
    out_ref,
    number_ref,
    *,
    width,
):
    value = pair_ref[...].astype(F32)
    average = jnp.mean(value, axis=-1, keepdims=True)
    centered = value - average
    variance = jnp.mean(centered * centered, axis=-1, keepdims=True)
    normed = (centered * lax.rsqrt(variance + EPS) * gain_ref[...] + bias_ref[...]).astype(BF16)
    normed_ref[...] = normed
    project(normed, pl.program_id(0), tokens_ref, mask_ref, left_ref, right_ref, out_ref, 0, width)
    size = mask_ref.shape[1] // 2
    low = jnp.sum(mask_ref[:, :size])
    high = jnp.sum(mask_ref[:, size:])
    number = len(SIZES) - 1
    for n in range(len(SIZES) - 2, -1, -1):
        few, main, rest = counts(SIZES[n], 2 * size)
        fits = (jnp.maximum(low, high) <= few) & (low + high <= main + rest)
        number = jnp.where(fits, n, number)
    number_ref[0] = number


def later_kernel(tokens_ref, mask_ref, normed_ref, left_ref, right_ref, out_ref, *, low, width):
    step = pl.program_id(0)
    project(normed_ref[...], step, tokens_ref, mask_ref, left_ref, right_ref, out_ref, low, width)


def gate_kernel(normed_ref, weight_ref, gate_ref):
    rows, cols, pair_width = normed_ref.shape
    half = jnp.asarray(0.5, BF16)
    proj = dot(normed_ref[...].reshape(rows * cols, pair_width), weight_ref[...] * half)
    gate_ref[...] = (0.5 * jnp.tanh(proj) + 0.5).reshape(gate_ref.shape)


def counts(sizes, tokens):
    few, main, rest = sizes
    return tokens // 2 * few // 16, tokens * main // 4, tokens * rest // 16


def places(valid):
    size = valid.shape[1]
    above = lax.broadcasted_iota(jnp.int32, (size, size), 0)
    below = lax.broadcasted_iota(jnp.int32, (size, size), 1)
    through = dot(valid.astype(BF16), jnp.where(above <= below, 1.0, 0.0).astype(BF16))
    return jnp.where(valid > 0.5, through - 1.0, -1.0)[:1]


def ones_at(place, targets):
    return jnp.where(targets.astype(F32) == place, 1.0, 0.0)


def picks_kernel(tokens_ref, all_ref, spread_ref, pick_ref, back_ref, *, main, rest, share):
    tokens = tokens_ref.shape[1]
    valid = jnp.broadcast_to(tokens_ref[...].astype(F32), (16, tokens))
    place = places(valid)
    lanes = spread_ref.shape[1]
    all_ref[...] = ones_at(
        place, lax.broadcasted_iota(jnp.int32, all_ref.shape, 0)
    ).astype(BF16)
    target = lax.broadcasted_iota(jnp.int32, (lanes, tokens), 0)
    if rest:
        pack = (lanes - main) // share
        past = target - main
        slot = lax.rem(jnp.maximum(past, 0), pack) - lax.div(jnp.maximum(past, 0), pack) * rest
        packed = jnp.where((slot >= 0) & (slot < rest), main + slot, -2)
        target = jnp.where(past >= 0, packed, target)
    spread_ref[...] = ones_at(place, target).T.astype(BF16)
    size = tokens // 2
    low, high = places(valid[:, :size]), places(valid[:, size:])
    second = own_half() == 1
    order = lax.broadcasted_iota(jnp.int32, pick_ref.shape, 0)
    pick_ref[...] = ones_at(jnp.where(second, low, high), order).astype(BF16)
    back_ref[...] = ones_at(jnp.where(second, high, low), order).T.astype(BF16)


def panel(ref, side, start, count):
    parts = []
    for h in range(ref.shape[3]):
        for z in range(ref.shape[1]):
            block = ref[pl.ds(start, count), z, side, h]
            parts.append(block.reshape(count * block.shape[1], block.shape[2]))
    return jnp.concatenate(parts, 1)


def own_half():
    return lax.axis_index("col") // (lax.axis_size("col") // 2)


def far_kernel(all_ref, pick_ref, edges_ref, far_ref, *, main, rest):
    devices, groups, _, share, rows, cols = edges_ref.shape
    depth = groups * cols
    left = panel(edges_ref, 0, 0, devices)
    right = panel(edges_ref, 1, (1 - own_half()) * (devices // 2), devices // 2)
    left = dot(all_ref[...], left).astype(BF16)
    right = dot(pick_ref[...], right).astype(BF16)
    for h in range(share):
        k = slice(h * depth, (h + 1) * depth)
        far_ref[:, h * main : (h + 1) * main] = dot(right[:, k], left[:main, k], NT).astype(BF16)
    if rest:
        pack = far_ref.shape[1] - share * main
        few = left[main:]
        few = jnp.concatenate(
            [few] * share + [jnp.zeros((pack - share * rest, few.shape[1]), BF16)]
            if pack > share * rest
            else [few] * share,
            0,
        )
        row_h = lax.broadcasted_iota(jnp.int32, few.shape, 0) // rest
        lane_h = lax.broadcasted_iota(jnp.int32, few.shape, 1) // depth
        few = jnp.where(row_h == lane_h, few, jnp.zeros_like(few))
        far_ref[:, share * main :] = dot(right, few, NT).astype(BF16)


def near_kernel(spread_ref, back_ref, edges_ref, far_ref, out_ref, *, main, rest):
    devices, groups, share, rows, cols = out_ref.shape
    depth = groups * cols
    left = panel(edges_ref, 0, 0, devices)
    right = panel(edges_ref, 1, own_half() * (devices // 2), devices // 2)
    wide = dot(back_ref[...], far_ref[...]).astype(BF16)
    pack = wide.shape[1] - share * main
    for h in range(share):
        k = slice(h * depth, (h + 1) * depth)
        here = [left[:, k], spread_ref[:, :main]]
        there = [right[:, k], wide[:, h * main : (h + 1) * main]]
        if rest:
            here.append(spread_ref[:, main + h * pack : main + (h + 1) * pack])
            there.append(wide[:, share * main :])
        total = dot(jnp.concatenate(here, 1), jnp.concatenate(there, 1), NT).astype(BF16)
        for z in range(groups):
            out_ref[:, z, h] = total[:, z * cols : (z + 1) * cols].reshape(devices, rows, cols)


def last_kernel(*refs):
    gate_ref, gain_ref, bias_ref, weight_ref = refs[:4]
    out_ref = refs[-1]
    rows, cols = gate_ref.shape[:2]
    hidden = weight_ref.shape[0]
    parts = []
    for ref in refs[4:-1]:
        parts.append(ref[...].reshape(ref.shape[0] * ref.shape[1], rows, cols))
    value = jnp.swapaxes(jnp.concatenate(parts, 0), 0, 1)
    weight = weight_ref[...]
    gain = jnp.broadcast_to(gain_ref[...], (cols, hidden)).T
    bias = jnp.broadcast_to(bias_ref[...], (cols, hidden)).T
    for i in range(rows):
        product = value[i].astype(F32)
        average = jnp.mean(product, axis=0, keepdims=True)
        centered = product - average
        variance = jnp.mean(centered * centered, axis=0, keepdims=True)
        normed = centered * lax.rsqrt(variance + EPS) * gain + bias
        update = dot(normed.astype(BF16), weight, (((0,), (0,)), ((), ())))
        out_ref[i] = (gate_ref[i] * update).astype(BF16)


def shards(
    pair_rep,
    token_mask,
    in_gain,
    in_bias,
    left_weight,
    right_weight,
    gate_weight,
    out_gain,
    out_bias,
    out_weight,
):
    rows, cols, pair_width = pair_rep.shape
    hidden = out_weight.shape[0]
    row_count = lax.axis_size("row")
    col_count = lax.axis_size("col")
    group_cols = col_count // 2
    members = row_count * group_cols
    share = hidden // members
    chunks = CHUNKS if share % CHUNKS == 0 else 1
    share //= chunks
    width = hidden // chunks
    tokens = row_count * rows
    near_tokens = group_cols * cols
    axes = ("row", "col")
    groups = [
        [r * col_count + h * group_cols + z for r in range(row_count) for z in range(group_cols)]
        for h in range(2)
    ]
    across = [(c, (c + group_cols) % col_count) for c in range(col_count)]

    tile = min(ROW_TILE, rows)
    steps = rows // tile
    by_row = lambda *tail: pl.BlockSpec((tile,) + tail, lambda i: (i,) + (0,) * len(tail))
    edge_shape = jax.ShapeDtypeStruct((members, 2, share, rows, cols), BF16)
    edge_spec = pl.BlockSpec((members, 2, share, tile, cols), lambda i: (0, 0, 0, i, 0))
    mask_row = token_mask[None]
    mask_specs = [pl.BlockSpec(memory_space=pltpu.SMEM), whole(mask_row)]
    weight_specs = [whole(left_weight), whole(right_weight)]
    normed, first, number = pl.pallas_call(
        functools.partial(first_kernel, width=width),
        grid=(steps,),
        in_specs=mask_specs
        + [by_row(cols, pair_width)]
        + weight_specs
        + [whole(in_gain[None]), whole(in_bias[None])],
        out_specs=[by_row(cols, pair_width), edge_spec, pl.BlockSpec(memory_space=pltpu.SMEM)],
        out_shape=[
            jax.ShapeDtypeStruct(pair_rep.shape, BF16),
            edge_shape,
            jax.ShapeDtypeStruct((1,), jnp.int32),
        ],
        compiler_params=PARAMS,
        name="norm_project",
    )(token_mask, mask_row, pair_rep, left_weight, right_weight, in_gain[None], in_bias[None])

    def after(value, others):
        return lax.optimization_barrier((value, *others))[0] if others else value

    def exchange(value):
        return lax.all_to_all(value, axes, 0, 0, axis_index_groups=groups, tiled=True)

    def middle(sizes, normed, first, token_mask):
        few, main, rest = counts(sizes, tokens)
        pack = -(-share * rest // 128) * 128
        lanes = share * main + pack
        mask_row = token_mask[None]
        all_pick, spread, pick, back_pick = pl.pallas_call(
            functools.partial(picks_kernel, main=main, rest=rest, share=share),
            out_shape=[
                jax.ShapeDtypeStruct((main + rest, tokens), BF16),
                jax.ShapeDtypeStruct((tokens, main + share * pack), BF16),
                jax.ShapeDtypeStruct((few, near_tokens), BF16),
                jax.ShapeDtypeStruct((near_tokens, few), BF16),
            ],
            compiler_params=PARAMS,
            cost_estimate=pl.CostEstimate(
                flops=64 * tokens * tokens, bytes_accessed=6 * tokens * tokens, transcendentals=0
            ),
            name="picks",
        )(mask_row)
        edges = [first]
        for t in range(1, chunks):
            edges.append(
                pl.pallas_call(
                    functools.partial(later_kernel, low=t * width, width=width),
                    grid=(steps,),
                    in_specs=mask_specs + [by_row(cols, pair_width)] + weight_specs,
                    out_specs=edge_spec,
                    out_shape=edge_shape,
                    compiler_params=PARAMS,
                    cost_estimate=pl.CostEstimate(
                        flops=4 * rows * cols * pair_width * width * 2,
                        bytes_accessed=3 * rows * cols * pair_width * 2,
                        transcendentals=rows * cols * width * 2,
                    ),
                    name="project",
                )(token_mask, mask_row, after(normed, [pick]), left_weight, right_weight)
            )
        gate = pl.pallas_call(
            gate_kernel,
            grid=(steps,),
            in_specs=[by_row(cols, pair_width), whole(gate_weight)],
            out_specs=by_row(cols, pair_width),
            out_shape=jax.ShapeDtypeStruct(pair_rep.shape, F32),
            compiler_params=PARAMS,
            cost_estimate=pl.CostEstimate(
                flops=2 * rows * cols * pair_width * pair_width,
                bytes_accessed=rows * cols * pair_width * 6,
                transcendentals=rows * cols * pair_width,
            ),
            name="gate",
        )(normed, gate_weight)

        product_bytes = share * tokens * near_tokens * 6
        arrived = []
        sent = []
        fars = []
        for t in range(chunks):
            edge = after(edges[t], arrived[-1:])
            here = exchange(edge).reshape(row_count, group_cols, 2, share, rows, cols)
            arrived.append(here)
            far = pl.pallas_call(
                functools.partial(far_kernel, main=main, rest=rest),
                out_shape=jax.ShapeDtypeStruct((few, lanes), BF16),
                compiler_params=PARAMS,
                cost_estimate=pl.CostEstimate(
                    flops=6 * share * tokens * near_tokens * near_tokens,
                    bytes_accessed=product_bytes,
                    transcendentals=0,
                ),
                name="far_product",
            )(all_pick, pick, here)
            sent.append(far)
            fars.append(lax.ppermute(far, "col", across))
        back = []
        totals = []
        for t in range(chunks):
            total = pl.pallas_call(
                functools.partial(near_kernel, main=main, rest=rest),
                out_shape=jax.ShapeDtypeStruct((row_count, group_cols, share, rows, cols), BF16),
                compiler_params=PARAMS,
                cost_estimate=pl.CostEstimate(
                    flops=NEAR_FLOPS, bytes_accessed=product_bytes, transcendentals=0
                ),
                name="near_product",
            )(spread, back_pick, arrived[t], after(fars[t], sent[t + 1 : t + 2] + totals[-1:]))
            totals.append(total)
            back.append(exchange(total.reshape(members, share, rows, cols)))
        return gate, *back

    branches = [functools.partial(middle, sizes) for sizes in SIZES]
    gate, *back = lax.switch(number[0], branches, normed, first, token_mask)
    piece = pl.BlockSpec((members, share, tile, cols), lambda i: (0, 0, i, 0))
    return pl.pallas_call(
        last_kernel,
        grid=(steps,),
        in_specs=[
            by_row(cols, pair_width),
            whole(out_gain[None]),
            whole(out_bias[None]),
            whole(out_weight),
        ]
        + [piece] * chunks,
        out_specs=by_row(cols, pair_width),
        out_shape=jax.ShapeDtypeStruct(pair_rep.shape, BF16),
        compiler_params=PARAMS,
        name="norm_out",
    )(gate, out_gain[None], out_bias[None], out_weight, *back)


def solution(mesh):
    placed = (P("row", "col", None), P(), P(), P(), P(), P(), P(), P(), P(), P())
    return jax.shard_map(
        shards, mesh=mesh, in_specs=placed, out_specs=P("row", "col", None), check_vma=False
    )
```

```python
import functools

import jax
import jax.numpy as jnp
from jax import lax
from jax.experimental import pallas as pl
from jax.experimental.pallas import tpu as pltpu
from jax.sharding import PartitionSpec as P

EPS = 1e-05
F32 = jnp.float32
BF16 = jnp.bfloat16
ROW_TILE = 32
CHUNKS = 2
NEAR_FLOPS = 2 * 10**10
PARAMS = pltpu.CompilerParams(vmem_limit_bytes=56 * 2**20)
SMALL = pltpu.CompilerParams(vmem_limit_bytes=24 * 2**20)
NT = (((1,), (1,)), ((), ()))
SIZES = ((12, 3, 0), (13, 3, 1), (14, 3, 1), (16, 4, 0))


def whole(array):
    return pl.BlockSpec(array.shape, lambda *_: (0,) * array.ndim)


def dot(left, right, dims=(((1,), (0,)), ((), ()))):
    return lax.dot_general(left, right, dims, preferred_element_type=F32)


def project(normed, tokens_ref, mask_ref, left_ref, right_ref, out_ref, low, width):
    rows, cols, pair_width = normed.shape
    hidden = left_ref.shape[1] // 2
    half = jnp.asarray(0.5, BF16)
    left = left_ref[...].T * half
    right = right_ref[...].T * half
    weight = jnp.concatenate(
        [
            left[low : low + width],
            right[low : low + width],
            left[hidden + low : hidden + low + width],
            right[hidden + low : hidden + low + width],
        ],
        0,
    )
    start = (lax.axis_index("row") * pl.num_programs(0) + pl.program_id(0)) * rows
    tokens = mask_ref.shape[1]
    valid = jnp.broadcast_to(mask_ref[...], (8, tokens)).astype(F32)
    valid = pltpu.roll(valid, lax.rem(tokens - lax.axis_index("col") * cols, tokens), 1)
    valid = valid[:1, :cols]
    pieces = []
    for i in range(0, rows, 2):
        two = normed[i : i + 2].reshape(2 * cols, pair_width)
        proj = dot(weight, two, NT)
        pair_valid = jnp.concatenate(
            [valid * tokens_ref[start + i + n].astype(F32) for n in range(2)], 1
        )
        value = (jnp.tanh(proj[: 2 * width]) + 1.0) * (proj[2 * width :] * pair_valid)
        value = value.astype(BF16)
        pieces += [value[:, :cols], value[:, cols:]]
    value = jnp.swapaxes(jnp.stack(pieces, 0), 0, 1)
    dests, _, share = out_ref.shape[:3]
    for side in range(2):
        part = value[side * width : (side + 1) * width]
        out_ref[:, side] = part.reshape(dests, share, rows, cols)


def normalise(pair_ref, gain_ref, bias_ref):
    rows, cols, pair_width = pair_ref.shape
    flat = pair_ref[...].reshape(rows * cols, pair_width)
    average = dot(flat, jnp.full((pair_width, pair_width), 1.0 / pair_width, BF16))
    centered = flat.astype(F32) - average
    variance = jnp.mean(centered * centered, axis=-1, keepdims=True)
    return (centered * lax.rsqrt(variance + EPS) * gain_ref[...] + bias_ref[...]).astype(BF16)


def first_kernel(
    tokens_ref, mask_ref, pair_ref, left_ref, right_ref, gain_ref, bias_ref, out_ref, number_ref, *, width
):
    normed = normalise(pair_ref, gain_ref, bias_ref).reshape(pair_ref.shape)
    project(normed, tokens_ref, mask_ref, left_ref, right_ref, out_ref, 0, width)
    size = mask_ref.shape[1] // 2
    low = jnp.sum(mask_ref[:, :size])
    high = jnp.sum(mask_ref[:, size:])
    number = len(SIZES) - 1
    for n in range(len(SIZES) - 2, -1, -1):
        few, main, rest = counts(SIZES[n], 2 * size)
        fits = (jnp.maximum(low, high) <= few) & (low + high <= main + rest)
        number = jnp.where(fits, n, number)
    number_ref[0] = number


def gate_kernel(*refs, low, width):
    tokens_ref, mask_ref, pair_ref, left_ref, right_ref, gain_ref, bias_ref, weight_ref = refs[:8]
    flat = normalise(pair_ref, gain_ref, bias_ref)
    half = jnp.asarray(0.5, BF16)
    proj = dot(flat, weight_ref[...] * half)
    refs[8][...] = (0.5 * jnp.tanh(proj) + 0.5).reshape(pair_ref.shape)
    if width:
        normed = flat.reshape(pair_ref.shape)
        project(normed, tokens_ref, mask_ref, left_ref, right_ref, refs[9], low, width)


def counts(sizes, tokens):
    few, main, rest = sizes
    return tokens // 2 * few // 16, tokens * main // 4, tokens * rest // 16


def places(valid):
    size = valid.shape[1]
    above = lax.broadcasted_iota(jnp.int32, (size, size), 0)
    below = lax.broadcasted_iota(jnp.int32, (size, size), 1)
    through = dot(valid.astype(BF16), jnp.where(above <= below, 1.0, 0.0).astype(BF16))
    return jnp.where(valid > 0.5, through - 1.0, -1.0)[:1]


def ones_at(place, targets):
    return jnp.where(targets.astype(F32) == place, 1.0, 0.0)


def picks_kernel(tokens_ref, all_ref, spread_ref, pick_ref, back_ref, *, main, rest, share):
    tokens = tokens_ref.shape[1]
    valid = jnp.broadcast_to(tokens_ref[...].astype(F32), (16, tokens))
    place = places(valid)
    lanes = spread_ref.shape[1]
    all_ref[...] = ones_at(
        place, lax.broadcasted_iota(jnp.int32, all_ref.shape, 0)
    ).astype(BF16)
    target = lax.broadcasted_iota(jnp.int32, (lanes, tokens), 0)
    if rest:
        pack = (lanes - main) // share
        past = target - main
        slot = lax.rem(jnp.maximum(past, 0), pack) - lax.div(jnp.maximum(past, 0), pack) * rest
        packed = jnp.where((slot >= 0) & (slot < rest), main + slot, -2)
        target = jnp.where(past >= 0, packed, target)
    spread_ref[...] = ones_at(place, target).T.astype(BF16)
    size = tokens // 2
    low, high = places(valid[:, :size]), places(valid[:, size:])
    second = own_half() == 1
    order = lax.broadcasted_iota(jnp.int32, pick_ref.shape, 0)
    pick_ref[...] = ones_at(jnp.where(second, low, high), order).astype(BF16)
    back_ref[...] = ones_at(jnp.where(second, high, low), order).T.astype(BF16)


def panel(ref, side, start, count):
    parts = []
    for h in range(ref.shape[3]):
        for z in range(ref.shape[1]):
            block = ref[pl.ds(start, count), z, side, h]
            parts.append(block.reshape(count * block.shape[1], block.shape[2]))
    return jnp.concatenate(parts, 1)


def own_half():
    return lax.axis_index("col") // (lax.axis_size("col") // 2)


def far_kernel(all_ref, pick_ref, edges_ref, far_ref, *, main, rest):
    devices, groups, _, share, rows, cols = edges_ref.shape
    depth = groups * cols
    left = panel(edges_ref, 0, 0, devices)
    right = panel(edges_ref, 1, (1 - own_half()) * (devices // 2), devices // 2)
    left = dot(all_ref[...], left).astype(BF16)
    right = dot(pick_ref[...], right).astype(BF16)
    for h in range(share):
        k = slice(h * depth, (h + 1) * depth)
        far_ref[:, h * main : (h + 1) * main] = dot(right[:, k], left[:main, k], NT).astype(BF16)
    if rest:
        pack = far_ref.shape[1] - share * main
        few = left[main:]
        few = jnp.concatenate(
            [few] * share + [jnp.zeros((pack - share * rest, few.shape[1]), BF16)]
            if pack > share * rest
            else [few] * share,
            0,
        )
        row_h = lax.broadcasted_iota(jnp.int32, few.shape, 0) // rest
        lane_h = lax.broadcasted_iota(jnp.int32, few.shape, 1) // depth
        few = jnp.where(row_h == lane_h, few, jnp.zeros_like(few))
        far_ref[:, share * main :] = dot(right, few, NT).astype(BF16)


def near_kernel(spread_ref, back_ref, edges_ref, far_ref, out_ref, *, main, rest):
    devices, groups, share, rows, cols = out_ref.shape
    depth = groups * cols
    left = panel(edges_ref, 0, 0, devices)
    right = panel(edges_ref, 1, own_half() * (devices // 2), devices // 2)
    wide = dot(back_ref[...], far_ref[...]).astype(BF16)
    pack = wide.shape[1] - share * main
    for h in range(share):
        k = slice(h * depth, (h + 1) * depth)
        here = [left[:, k], spread_ref[:, :main]]
        there = [right[:, k], wide[:, h * main : (h + 1) * main]]
        if rest:
            here.append(spread_ref[:, main + h * pack : main + (h + 1) * pack])
            there.append(wide[:, share * main :])
        total = dot(jnp.concatenate(here, 1), jnp.concatenate(there, 1), NT).astype(BF16)
        for z in range(groups):
            out_ref[:, z, h] = total[:, z * cols : (z + 1) * cols].reshape(devices, rows, cols)


def last_kernel(*refs):
    gate_ref, gain_ref, bias_ref, weight_ref = refs[:4]
    out_ref = refs[-1]
    rows, cols = gate_ref.shape[:2]
    hidden = weight_ref.shape[0]
    parts = []
    for ref in refs[4:-1]:
        parts.append(ref[...].reshape(ref.shape[0] * ref.shape[1], rows, cols))
    value = jnp.swapaxes(jnp.concatenate(parts, 0), 0, 1)
    weight = weight_ref[...]
    gain = jnp.broadcast_to(gain_ref[...], (cols, hidden)).T
    bias = jnp.broadcast_to(bias_ref[...], (cols, hidden)).T
    for i in range(rows):
        product = value[i].astype(F32)
        average = jnp.mean(product, axis=0, keepdims=True)
        centered = product - average
        variance = jnp.mean(centered * centered, axis=0, keepdims=True)
        normed = centered * lax.rsqrt(variance + EPS) * gain + bias
        update = dot(normed.astype(BF16), weight, (((0,), (0,)), ((), ())))
        out_ref[i] = (gate_ref[i] * update).astype(BF16)


def shards(
    pair_rep,
    token_mask,
    in_gain,
    in_bias,
    left_weight,
    right_weight,
    gate_weight,
    out_gain,
    out_bias,
    out_weight,
):
    rows, cols, pair_width = pair_rep.shape
    hidden = out_weight.shape[0]
    row_count = lax.axis_size("row")
    col_count = lax.axis_size("col")
    group_cols = col_count // 2
    members = row_count * group_cols
    share = hidden // members
    chunks = CHUNKS if share % CHUNKS == 0 else 1
    share //= chunks
    width = hidden // chunks
    tokens = row_count * rows
    near_tokens = group_cols * cols
    axes = ("row", "col")
    groups = [
        [r * col_count + h * group_cols + z for r in range(row_count) for z in range(group_cols)]
        for h in range(2)
    ]
    across = [(c, (c + group_cols) % col_count) for c in range(col_count)]

    tile = min(ROW_TILE, rows)
    steps = rows // tile
    by_row = lambda *tail: pl.BlockSpec((tile,) + tail, lambda i: (i,) + (0,) * len(tail))
    edge_shape = jax.ShapeDtypeStruct((members, 2, share, rows, cols), BF16)
    edge_spec = pl.BlockSpec((members, 2, share, tile, cols), lambda i: (0, 0, 0, i, 0))
    mask_row = token_mask[None]
    mask_specs = [pl.BlockSpec(memory_space=pltpu.SMEM), whole(mask_row)]
    weight_specs = [whole(left_weight), whole(right_weight)]
    operands = (token_mask, mask_row, pair_rep, left_weight, right_weight)
    operands += (in_gain[None], in_bias[None])
    operand_specs = (
        mask_specs
        + [by_row(cols, pair_width)]
        + weight_specs
        + [whole(in_gain[None]), whole(in_bias[None])]
    )
    first, number = pl.pallas_call(
        functools.partial(first_kernel, width=width),
        grid=(steps,),
        in_specs=operand_specs,
        out_specs=[edge_spec, pl.BlockSpec(memory_space=pltpu.SMEM)],
        out_shape=[edge_shape, jax.ShapeDtypeStruct((1,), jnp.int32)],
        compiler_params=PARAMS,
        name="norm_project",
    )(*operands)

    def after(value, others):
        return lax.optimization_barrier((value, *others))[0] if others else value

    def exchange(value):
        return lax.all_to_all(value, axes, 0, 0, axis_index_groups=groups, tiled=True)

    def middle(sizes, first, token_mask, pair_rep):
        few, main, rest = counts(sizes, tokens)
        pack = -(-share * rest // 128) * 128
        lanes = share * main + pack
        mask_row = token_mask[None]
        all_pick, spread, pick, back_pick = pl.pallas_call(
            functools.partial(picks_kernel, main=main, rest=rest, share=share),
            out_shape=[
                jax.ShapeDtypeStruct((main + rest, tokens), BF16),
                jax.ShapeDtypeStruct((tokens, main + share * pack), BF16),
                jax.ShapeDtypeStruct((few, near_tokens), BF16),
                jax.ShapeDtypeStruct((near_tokens, few), BF16),
            ],
            compiler_params=SMALL,
            cost_estimate=pl.CostEstimate(
                flops=64 * tokens * tokens, bytes_accessed=6 * tokens * tokens, transcendentals=0
            ),
            name="picks",
        )(mask_row)
        gate_shape = jax.ShapeDtypeStruct(pair_rep.shape, F32)
        gate, *edges = pl.pallas_call(
            functools.partial(gate_kernel, low=width, width=width * (chunks - 1)),
            grid=(steps,),
            in_specs=operand_specs + [whole(gate_weight)],
            out_specs=[by_row(cols, pair_width)] + [edge_spec] * (chunks - 1),
            out_shape=[gate_shape] + [edge_shape] * (chunks - 1),
            compiler_params=PARAMS,
            cost_estimate=pl.CostEstimate(
                flops=12 * rows * cols * pair_width * pair_width,
                bytes_accessed=10 * rows * cols * pair_width,
                transcendentals=3 * rows * cols * pair_width,
            ),
            name="gate_project",
        )(*operands[:2], after(pair_rep, [pick]), *operands[3:], gate_weight)
        edges = [first] + edges

        product_bytes = share * tokens * near_tokens * 6
        arrived = []
        sent = []
        fars = []
        for t in range(chunks):
            edge = after(edges[t], arrived[-1:])
            here = exchange(edge).reshape(row_count, group_cols, 2, share, rows, cols)
            arrived.append(here)
            far = pl.pallas_call(
                functools.partial(far_kernel, main=main, rest=rest),
                out_shape=jax.ShapeDtypeStruct((few, lanes), BF16),
                compiler_params=SMALL,
                cost_estimate=pl.CostEstimate(
                    flops=6 * share * tokens * near_tokens * near_tokens,
                    bytes_accessed=product_bytes,
                    transcendentals=0,
                ),
                name="far_product",
            )(all_pick, pick, here)
            sent.append(far)
            fars.append(lax.ppermute(far, "col", across))
        back = []
        totals = []
        for t in range(chunks):
            total = pl.pallas_call(
                functools.partial(near_kernel, main=main, rest=rest),
                out_shape=jax.ShapeDtypeStruct((row_count, group_cols, share, rows, cols), BF16),
                compiler_params=SMALL,
                cost_estimate=pl.CostEstimate(
                    flops=NEAR_FLOPS, bytes_accessed=product_bytes, transcendentals=0
                ),
                name="near_product",
            )(spread, back_pick, arrived[t], after(fars[t], sent[t + 1 : t + 2] + totals[-1:]))
            totals.append(total)
            back.append(exchange(total.reshape(members, share, rows, cols)))
        return gate, *back

    branches = [functools.partial(middle, sizes) for sizes in SIZES]
    gate, *back = lax.switch(number[0], branches, first, token_mask, pair_rep)
    piece = pl.BlockSpec((members, share, tile, cols), lambda i: (0, 0, i, 0))
    return pl.pallas_call(
        last_kernel,
        grid=(steps,),
        in_specs=[
            by_row(cols, pair_width),
            whole(out_gain[None]),
            whole(out_bias[None]),
            whole(out_weight),
        ]
        + [piece] * chunks,
        out_specs=by_row(cols, pair_width),
        out_shape=jax.ShapeDtypeStruct(pair_rep.shape, BF16),
        compiler_params=SMALL,
        name="norm_out",
    )(gate, out_gain[None], out_bias[None], out_weight, *back)


def solution(mesh):
    placed = (P("row", "col", None), P(), P(), P(), P(), P(), P(), P(), P(), P())
    return jax.shard_map(
        shards, mesh=mesh, in_specs=placed, out_specs=P("row", "col", None), check_vma=False
    )
```

```python
import functools

import jax
import jax.numpy as jnp
from jax import lax
from jax.experimental import pallas as pl
from jax.experimental.pallas import tpu as pltpu
from jax.sharding import PartitionSpec as P

EPS = 1e-05
F32 = jnp.float32
BF16 = jnp.bfloat16
ROW_TILE = 32
CHUNKS = 2
NEAR_FLOPS = 2 * 10**10
PARAMS = pltpu.CompilerParams(vmem_limit_bytes=56 * 2**20)
SMALL = pltpu.CompilerParams(vmem_limit_bytes=24 * 2**20)
NT = (((1,), (1,)), ((), ()))
SIZES = ((12, 3, 0), (13, 3, 0), (13, 3, 1), (14, 3, 1), (16, 4, 0))


def whole(array):
    return pl.BlockSpec(array.shape, lambda *_: (0,) * array.ndim)


def dot(left, right, dims=(((1,), (0,)), ((), ()))):
    return lax.dot_general(left, right, dims, preferred_element_type=F32)


def project(normed, tokens_ref, mask_ref, left_ref, right_ref, out_ref, low, width):
    rows, cols, pair_width = normed.shape
    hidden = left_ref.shape[1] // 2
    half = jnp.asarray(0.5, BF16)
    left = left_ref[...].T * half
    right = right_ref[...].T * half
    weight = jnp.concatenate(
        [
            left[low : low + width],
            right[low : low + width],
            left[hidden + low : hidden + low + width],
            right[hidden + low : hidden + low + width],
        ],
        0,
    )
    start = (lax.axis_index("row") * pl.num_programs(0) + pl.program_id(0)) * rows
    tokens = mask_ref.shape[1]
    valid = jnp.broadcast_to(mask_ref[...], (8, tokens)).astype(F32)
    valid = pltpu.roll(valid, lax.rem(tokens - lax.axis_index("col") * cols, tokens), 1)
    valid = valid[:1, :cols]
    pieces = []
    for i in range(0, rows, 2):
        two = normed[i : i + 2].reshape(2 * cols, pair_width)
        proj = dot(weight, two, NT)
        pair_valid = jnp.concatenate(
            [valid * tokens_ref[start + i + n].astype(F32) for n in range(2)], 1
        )
        value = (jnp.tanh(proj[: 2 * width]) + 1.0) * (proj[2 * width :] * pair_valid)
        value = value.astype(BF16)
        pieces += [value[:, :cols], value[:, cols:]]
    value = jnp.swapaxes(jnp.stack(pieces, 0), 0, 1)
    dests, _, share = out_ref.shape[:3]
    for side in range(2):
        part = value[side * width : (side + 1) * width]
        out_ref[:, side] = part.reshape(dests, share, rows, cols)


def normalise(pair_ref, gain_ref, bias_ref):
    rows, cols, pair_width = pair_ref.shape
    flat = pair_ref[...].reshape(rows * cols, pair_width)
    average = dot(flat, jnp.full((pair_width, pair_width), 1.0 / pair_width, BF16))
    centered = flat.astype(F32) - average
    variance = jnp.mean(centered * centered, axis=-1, keepdims=True)
    return (centered * lax.rsqrt(variance + EPS) * gain_ref[...] + bias_ref[...]).astype(BF16)


def first_kernel(
    tokens_ref, mask_ref, pair_ref, left_ref, right_ref, gain_ref, bias_ref, out_ref, number_ref, *, width
):
    normed = normalise(pair_ref, gain_ref, bias_ref).reshape(pair_ref.shape)
    project(normed, tokens_ref, mask_ref, left_ref, right_ref, out_ref, 0, width)
    size = mask_ref.shape[1] // 2
    low = jnp.sum(mask_ref[:, :size])
    high = jnp.sum(mask_ref[:, size:])
    number = len(SIZES) - 1
    for n in range(len(SIZES) - 2, -1, -1):
        few, main, rest = counts(SIZES[n], 2 * size)
        fits = (jnp.maximum(low, high) <= few) & (low + high <= main + rest)
        number = jnp.where(fits, n, number)
    number_ref[0] = number


def gate_kernel(*refs, low, width):
    tokens_ref, mask_ref, pair_ref, left_ref, right_ref, gain_ref, bias_ref, weight_ref = refs[:8]
    flat = normalise(pair_ref, gain_ref, bias_ref)
    half = jnp.asarray(0.5, BF16)
    proj = dot(flat, weight_ref[...] * half)
    refs[8][...] = (0.5 * jnp.tanh(proj) + 0.5).reshape(pair_ref.shape)
    if width:
        normed = flat.reshape(pair_ref.shape)
        project(normed, tokens_ref, mask_ref, left_ref, right_ref, refs[9], low, width)


def counts(sizes, tokens):
    few, main, rest = sizes
    return tokens // 2 * few // 16, tokens * main // 4, tokens * rest // 16


def places(valid):
    size = valid.shape[1]
    above = lax.broadcasted_iota(jnp.int32, (size, size), 0)
    below = lax.broadcasted_iota(jnp.int32, (size, size), 1)
    through = dot(valid.astype(BF16), jnp.where(above <= below, 1.0, 0.0).astype(BF16))
    return jnp.where(valid > 0.5, through - 1.0, -1.0)[:1]


def ones_at(place, targets):
    return jnp.where(targets.astype(F32) == place, 1.0, 0.0)


def picks_kernel(tokens_ref, all_ref, spread_ref, pick_ref, back_ref, *, share):
    tokens = tokens_ref.shape[1]
    valid = jnp.broadcast_to(tokens_ref[...].astype(F32), (16, tokens))
    place = places(valid)
    order = lax.broadcasted_iota(jnp.int32, all_ref.shape, 0)
    chosen = ones_at(place, order)
    all_ref[...] = chosen.astype(BF16)
    spread_ref[:, :tokens] = chosen.T.astype(BF16)
    _, main, rest = counts((0, 3, 1), tokens)
    pack = pack_of(share, rest)
    for h in range(share):
        slot = lax.broadcasted_iota(jnp.int32, (pack, tokens), 0) - h * rest
        target = jnp.where((slot >= 0) & (slot < rest), main + slot, -2)
        at = tokens + h * pack
        spread_ref[:, at : at + pack] = ones_at(place, target).T.astype(BF16)
    size = tokens // 2
    low, high = places(valid[:, :size]), places(valid[:, size:])
    second = own_half() == 1
    order = lax.broadcasted_iota(jnp.int32, pick_ref.shape, 0)
    pick_ref[...] = ones_at(jnp.where(second, low, high), order).astype(BF16)
    back_ref[...] = ones_at(jnp.where(second, high, low), order).T.astype(BF16)


def pack_of(share, rest):
    return -(-share * rest // 128) * 128


def panel(ref, side, start, count):
    parts = []
    for h in range(ref.shape[3]):
        for z in range(ref.shape[1]):
            block = ref[pl.ds(start, count), z, side, h]
            parts.append(block.reshape(count * block.shape[1], block.shape[2]))
    return jnp.concatenate(parts, 1)


def own_half():
    return lax.axis_index("col") // (lax.axis_size("col") // 2)


def far_kernel(all_ref, pick_ref, edges_ref, far_ref, *, main, rest):
    devices, groups, _, share, rows, cols = edges_ref.shape
    depth = groups * cols
    left = panel(edges_ref, 0, 0, devices)
    right = panel(edges_ref, 1, (1 - own_half()) * (devices // 2), devices // 2)
    left = dot(all_ref[: main + rest], left).astype(BF16)
    right = dot(pick_ref[: far_ref.shape[0]], right).astype(BF16)
    for h in range(share):
        k = slice(h * depth, (h + 1) * depth)
        far_ref[:, h * main : (h + 1) * main] = dot(right[:, k], left[:main, k], NT).astype(BF16)
    if rest:
        pack = far_ref.shape[1] - share * main
        few = left[main:]
        few = jnp.concatenate(
            [few] * share + [jnp.zeros((pack - share * rest, few.shape[1]), BF16)]
            if pack > share * rest
            else [few] * share,
            0,
        )
        row_h = lax.broadcasted_iota(jnp.int32, few.shape, 0) // rest
        lane_h = lax.broadcasted_iota(jnp.int32, few.shape, 1) // depth
        few = jnp.where(row_h == lane_h, few, jnp.zeros_like(few))
        far_ref[:, share * main :] = dot(right, few, NT).astype(BF16)


def near_kernel(spread_ref, back_ref, edges_ref, far_ref, out_ref, *, main, rest):
    devices, groups, share, rows, cols = out_ref.shape
    depth = groups * cols
    left = panel(edges_ref, 0, 0, devices)
    right = panel(edges_ref, 1, own_half() * (devices // 2), devices // 2)
    wide = dot(back_ref[:, : far_ref.shape[0]], far_ref[...]).astype(BF16)
    pack = wide.shape[1] - share * main
    tokens = devices * rows
    for h in range(share):
        k = slice(h * depth, (h + 1) * depth)
        here = [left[:, k], spread_ref[:, :main]]
        there = [right[:, k], wide[:, h * main : (h + 1) * main]]
        if rest:
            here.append(spread_ref[:, tokens + h * pack : tokens + (h + 1) * pack])
            there.append(wide[:, share * main :])
        total = dot(jnp.concatenate(here, 1), jnp.concatenate(there, 1), NT).astype(BF16)
        for z in range(groups):
            out_ref[:, z, h] = total[:, z * cols : (z + 1) * cols].reshape(devices, rows, cols)


def last_kernel(*refs):
    gate_ref, gain_ref, bias_ref, weight_ref = refs[:4]
    out_ref = refs[-1]
    rows, cols = gate_ref.shape[:2]
    hidden = weight_ref.shape[0]
    parts = []
    for ref in refs[4:-1]:
        parts.append(ref[...].reshape(ref.shape[0] * ref.shape[1], rows, cols))
    value = jnp.swapaxes(jnp.concatenate(parts, 0), 0, 1)
    weight = weight_ref[...]
    gain = jnp.broadcast_to(gain_ref[...], (cols, hidden)).T
    bias = jnp.broadcast_to(bias_ref[...], (cols, hidden)).T
    for i in range(rows):
        product = value[i].astype(F32)
        average = jnp.mean(product, axis=0, keepdims=True)
        centered = product - average
        variance = jnp.mean(centered * centered, axis=0, keepdims=True)
        normed = centered * lax.rsqrt(variance + EPS) * gain + bias
        update = dot(normed.astype(BF16), weight, (((0,), (0,)), ((), ())))
        out_ref[i] = (gate_ref[i] * update).astype(BF16)


def shards(
    pair_rep,
    token_mask,
    in_gain,
    in_bias,
    left_weight,
    right_weight,
    gate_weight,
    out_gain,
    out_bias,
    out_weight,
):
    rows, cols, pair_width = pair_rep.shape
    hidden = out_weight.shape[0]
    row_count = lax.axis_size("row")
    col_count = lax.axis_size("col")
    group_cols = col_count // 2
    members = row_count * group_cols
    share = hidden // members
    chunks = CHUNKS if share % CHUNKS == 0 else 1
    share //= chunks
    width = hidden // chunks
    tokens = row_count * rows
    near_tokens = group_cols * cols
    axes = ("row", "col")
    groups = [
        [r * col_count + h * group_cols + z for r in range(row_count) for z in range(group_cols)]
        for h in range(2)
    ]
    across = [(c, (c + group_cols) % col_count) for c in range(col_count)]

    tile = min(ROW_TILE, rows)
    steps = rows // tile
    by_row = lambda *tail: pl.BlockSpec((tile,) + tail, lambda i: (i,) + (0,) * len(tail))
    edge_shape = jax.ShapeDtypeStruct((members, 2, share, rows, cols), BF16)
    edge_spec = pl.BlockSpec((members, 2, share, tile, cols), lambda i: (0, 0, 0, i, 0))
    mask_row = token_mask[None]
    mask_specs = [pl.BlockSpec(memory_space=pltpu.SMEM), whole(mask_row)]
    weight_specs = [whole(left_weight), whole(right_weight)]
    operands = (token_mask, mask_row, pair_rep, left_weight, right_weight)
    operands += (in_gain[None], in_bias[None])
    operand_specs = (
        mask_specs
        + [by_row(cols, pair_width)]
        + weight_specs
        + [whole(in_gain[None]), whole(in_bias[None])]
    )
    first, number = pl.pallas_call(
        functools.partial(first_kernel, width=width),
        grid=(steps,),
        in_specs=operand_specs,
        out_specs=[edge_spec, pl.BlockSpec(memory_space=pltpu.SMEM)],
        out_shape=[edge_shape, jax.ShapeDtypeStruct((1,), jnp.int32)],
        compiler_params=PARAMS,
        name="norm_project",
    )(*operands)

    def after(value, others):
        return lax.optimization_barrier((value, *others))[0] if others else value

    def exchange(value):
        return lax.all_to_all(value, axes, 0, 0, axis_index_groups=groups, tiled=True)

    all_pick, spread, pick, back_pick = pl.pallas_call(
        functools.partial(picks_kernel, share=share),
        out_shape=[
            jax.ShapeDtypeStruct((tokens, tokens), BF16),
            jax.ShapeDtypeStruct((tokens, tokens + share * pack_of(share, tokens // 16)), BF16),
            jax.ShapeDtypeStruct((near_tokens, near_tokens), BF16),
            jax.ShapeDtypeStruct((near_tokens, near_tokens), BF16),
        ],
        compiler_params=SMALL,
        cost_estimate=pl.CostEstimate(
            flops=64 * tokens * tokens, bytes_accessed=6 * tokens * tokens, transcendentals=0
        ),
        name="picks",
    )(mask_row)
    gate_shape = jax.ShapeDtypeStruct(pair_rep.shape, F32)
    gate, *edges = pl.pallas_call(
        functools.partial(gate_kernel, low=width, width=width * (chunks - 1)),
        grid=(steps,),
        in_specs=operand_specs + [whole(gate_weight)],
        out_specs=[by_row(cols, pair_width)] + [edge_spec] * (chunks - 1),
        out_shape=[gate_shape] + [edge_shape] * (chunks - 1),
        compiler_params=PARAMS,
        cost_estimate=pl.CostEstimate(
            flops=12 * rows * cols * pair_width * pair_width,
            bytes_accessed=10 * rows * cols * pair_width,
            transcendentals=3 * rows * cols * pair_width,
        ),
        name="gate_project",
    )(*operands[:2], after(pair_rep, [first, pick]), *operands[3:], gate_weight)
    arrived0 = exchange(first)
    arrived0, *edges = lax.optimization_barrier((arrived0, *edges))

    def middle(sizes, arrived0, edges, all_pick, spread, pick, back_pick):
        few, main, rest = counts(sizes, tokens)
        lanes = share * main + pack_of(share, rest)
        product_bytes = share * tokens * near_tokens * 6
        arrived = []
        sent = []
        fars = []
        for t in range(chunks):
            here = exchange(after(edges[t - 1], arrived[-1:])) if t else arrived0
            here = here.reshape(row_count, group_cols, 2, share, rows, cols)
            arrived.append(here)
            far = pl.pallas_call(
                functools.partial(far_kernel, main=main, rest=rest),
                out_shape=jax.ShapeDtypeStruct((few, lanes), BF16),
                compiler_params=SMALL,
                cost_estimate=pl.CostEstimate(
                    flops=6 * share * tokens * near_tokens * near_tokens,
                    bytes_accessed=product_bytes,
                    transcendentals=0,
                ),
                name="far_product",
            )(all_pick, pick, here)
            sent.append(far)
            fars.append(lax.ppermute(far, "col", across))
        back = []
        totals = []
        for t in range(chunks):
            total = pl.pallas_call(
                functools.partial(near_kernel, main=main, rest=rest),
                out_shape=jax.ShapeDtypeStruct((row_count, group_cols, share, rows, cols), BF16),
                compiler_params=SMALL,
                cost_estimate=pl.CostEstimate(
                    flops=NEAR_FLOPS, bytes_accessed=product_bytes, transcendentals=0
                ),
                name="near_product",
            )(spread, back_pick, arrived[t], after(fars[t], sent[t + 1 : t + 2] + totals[-1:]))
            totals.append(total.reshape(members, share, rows, cols))
            if t < chunks - 1:
                back.append(exchange(totals[-1]))
        return *back, totals[-1]

    branches = [functools.partial(middle, sizes) for sizes in SIZES]
    *back, total = lax.switch(
        number[0], branches, arrived0, edges, all_pick, spread, pick, back_pick
    )
    back.append(exchange(total))
    piece = pl.BlockSpec((members, share, tile, cols), lambda i: (0, 0, i, 0))
    return pl.pallas_call(
        last_kernel,
        grid=(steps,),
        in_specs=[
            by_row(cols, pair_width),
            whole(out_gain[None]),
            whole(out_bias[None]),
            whole(out_weight),
        ]
        + [piece] * chunks,
        out_specs=by_row(cols, pair_width),
        out_shape=jax.ShapeDtypeStruct(pair_rep.shape, BF16),
        compiler_params=PARAMS,
        name="norm_out",
    )(gate, out_gain[None], out_bias[None], out_weight, *back)


def solution(mesh):
    placed = (P("row", "col", None), P(), P(), P(), P(), P(), P(), P(), P(), P())
    return jax.shard_map(
        shards, mesh=mesh, in_specs=placed, out_specs=P("row", "col", None), check_vma=False
    )
```

```python
import functools

import jax
import jax.numpy as jnp
from jax import lax
from jax.experimental import pallas as pl
from jax.experimental.pallas import tpu as pltpu
from jax.sharding import PartitionSpec as P

EPS = 1e-05
F32 = jnp.float32
BF16 = jnp.bfloat16
ROW_TILE = 32
CHUNKS = 2
NEAR_FLOPS = 2 * 10**10
PARAMS = pltpu.CompilerParams(vmem_limit_bytes=56 * 2**20)
SMALL = pltpu.CompilerParams(vmem_limit_bytes=24 * 2**20)
NT = (((1,), (1,)), ((), ()))
SIZES = ((12, 0), (13, 0), (13, 1), (14, 1), (15, 2), (16, 4))


def whole(array):
    return pl.BlockSpec(array.shape, lambda *_: (0,) * array.ndim)


def dot(left, right, dims=(((1,), (0,)), ((), ()))):
    return lax.dot_general(left, right, dims, preferred_element_type=F32)


def project(normed, tokens_ref, mask_ref, left_ref, right_ref, out_ref, low, width):
    rows, cols, pair_width = normed.shape
    hidden = left_ref.shape[1] // 2
    half = jnp.asarray(0.5, BF16)
    left = left_ref[...].T * half
    right = right_ref[...].T * half
    weight = jnp.concatenate(
        [
            left[low : low + width],
            right[low : low + width],
            left[hidden + low : hidden + low + width],
            right[hidden + low : hidden + low + width],
        ],
        0,
    )
    start = (lax.axis_index("row") * pl.num_programs(0) + pl.program_id(0)) * rows
    tokens = mask_ref.shape[1]
    valid = jnp.broadcast_to(mask_ref[...], (8, tokens)).astype(F32)
    valid = pltpu.roll(valid, lax.rem(tokens - lax.axis_index("col") * cols, tokens), 1)
    valid = valid[:1, :cols]
    pieces = []
    for i in range(0, rows, 2):
        two = normed[i : i + 2].reshape(2 * cols, pair_width)
        proj = dot(weight, two, NT)
        pair_valid = jnp.concatenate(
            [valid * tokens_ref[start + i + n].astype(F32) for n in range(2)], 1
        )
        value = (jnp.tanh(proj[: 2 * width]) + 1.0) * (proj[2 * width :] * pair_valid)
        value = value.astype(BF16)
        pieces += [value[:, :cols], value[:, cols:]]
    value = jnp.swapaxes(jnp.stack(pieces, 0), 0, 1)
    dests, _, share = out_ref.shape[:3]
    for side in range(2):
        part = value[side * width : (side + 1) * width]
        out_ref[:, side] = part.reshape(dests, share, rows, cols)


def normalise(pair_ref, gain_ref, bias_ref):
    rows, cols, pair_width = pair_ref.shape
    flat = pair_ref[...].reshape(rows * cols, pair_width)
    average = dot(flat, jnp.full((pair_width, pair_width), 1.0 / pair_width, BF16))
    centered = flat.astype(F32) - average
    variance = jnp.mean(centered * centered, axis=-1, keepdims=True)
    return (centered * lax.rsqrt(variance + EPS) * gain_ref[...] + bias_ref[...]).astype(BF16)


def first_kernel(
    tokens_ref, mask_ref, pair_ref, left_ref, right_ref, gain_ref, bias_ref, out_ref, number_ref, *, width
):
    normed = normalise(pair_ref, gain_ref, bias_ref).reshape(pair_ref.shape)
    project(normed, tokens_ref, mask_ref, left_ref, right_ref, out_ref, 0, width)
    size = mask_ref.shape[1] // 2
    low = jnp.sum(mask_ref[:, :size])
    high = jnp.sum(mask_ref[:, size:])
    number = len(SIZES) - 1
    for n in range(len(SIZES) - 2, -1, -1):
        few, main, rest = counts(SIZES[n], 2 * size)
        fits = (jnp.maximum(low, high) <= few) & (low + high <= main + sum(rest))
        number = jnp.where(fits, n, number)
    number_ref[0] = number


def gate_kernel(*refs, low, width):
    tokens_ref, mask_ref, pair_ref, left_ref, right_ref, gain_ref, bias_ref, weight_ref = refs[:8]
    flat = normalise(pair_ref, gain_ref, bias_ref)
    half = jnp.asarray(0.5, BF16)
    proj = dot(flat, weight_ref[...] * half)
    refs[8][...] = (0.5 * jnp.tanh(proj) + 0.5).reshape(pair_ref.shape)
    if width:
        normed = flat.reshape(pair_ref.shape)
        project(normed, tokens_ref, mask_ref, left_ref, right_ref, refs[9], low, width)


def counts(sizes, tokens):
    few, units = sizes
    return tokens // 2 * few // 16, tokens * 3 // 4, [tokens // 16] * units


def places(valid):
    size = valid.shape[1]
    above = lax.broadcasted_iota(jnp.int32, (size, size), 0)
    below = lax.broadcasted_iota(jnp.int32, (size, size), 1)
    through = dot(valid.astype(BF16), jnp.where(above <= below, 1.0, 0.0).astype(BF16))
    return jnp.where(valid > 0.5, through - 1.0, -1.0)[:1]


def ones_at(place, targets):
    return jnp.where(targets.astype(F32) == place, 1.0, 0.0)


def picks_kernel(tokens_ref, all_ref, pick_ref, back_ref, spread_ref, *rest_refs):
    tokens = tokens_ref.shape[1]
    valid = jnp.broadcast_to(tokens_ref[...].astype(F32), (16, tokens))
    place = places(valid)
    chosen = ones_at(place, lax.broadcasted_iota(jnp.int32, all_ref.shape, 0))
    all_ref[...] = chosen.astype(BF16)
    main = spread_ref.shape[1]
    spread_ref[...] = chosen[:main].T.astype(BF16)
    rest = (tokens - main) // len(rest_refs)
    for u, ref in enumerate(rest_refs):
        for h in range(ref.shape[0]):
            slot = lax.broadcasted_iota(jnp.int32, (ref.shape[2], tokens), 0) - h * rest
            target = jnp.where((slot >= 0) & (slot < rest), main + u * rest + slot, -2)
            ref[h] = ones_at(place, target).T.astype(BF16)
    size = tokens // 2
    low, high = places(valid[:, :size]), places(valid[:, size:])
    second = own_half() == 1
    order = lax.broadcasted_iota(jnp.int32, pick_ref.shape, 0)
    pick_ref[...] = ones_at(jnp.where(second, low, high), order).astype(BF16)
    back_ref[...] = ones_at(jnp.where(second, high, low), order).T.astype(BF16)


def pack_of(share, rest):
    return -(-share * rest // 128) * 128


def panel(ref, side, start, count):
    parts = []
    for h in range(ref.shape[3]):
        for z in range(ref.shape[1]):
            block = ref[pl.ds(start, count), z, side, h]
            parts.append(block.reshape(count * block.shape[1], block.shape[2]))
    return jnp.concatenate(parts, 1)


def own_half():
    return lax.axis_index("col") // (lax.axis_size("col") // 2)


def far_kernel(all_ref, pick_ref, edges_ref, far_ref, *, main, rest):
    devices, groups, _, share, rows, cols = edges_ref.shape
    depth = groups * cols
    left = panel(edges_ref, 0, 0, devices)
    right = panel(edges_ref, 1, (1 - own_half()) * (devices // 2), devices // 2)
    left = dot(all_ref[: main + sum(rest)], left).astype(BF16)
    right = dot(pick_ref[: far_ref.shape[0]], right).astype(BF16)
    for h in range(share):
        k = slice(h * depth, (h + 1) * depth)
        far_ref[:, h * main : (h + 1) * main] = dot(right[:, k], left[:main, k], NT).astype(BF16)
    at = share * main
    for u, size in enumerate(rest):
        few = left[main + u * size : main + (u + 1) * size]
        pack = pack_of(share, size)
        few = [few] * share
        if pack > share * size:
            few.append(jnp.zeros((pack - share * size, left.shape[1]), BF16))
        few = jnp.concatenate(few, 0)
        row_h = lax.broadcasted_iota(jnp.int32, few.shape, 0) // size
        lane_h = lax.broadcasted_iota(jnp.int32, few.shape, 1) // depth
        few = jnp.where(row_h == lane_h, few, jnp.zeros_like(few))
        far_ref[:, at : at + pack] = dot(right, few, NT).astype(BF16)
        at += pack


def near_kernel(back_ref, edges_ref, far_ref, spread_ref, *refs):
    out_ref = refs[-1]
    devices, groups, share, rows, cols = out_ref.shape
    depth = groups * cols
    main = spread_ref.shape[1]
    left = panel(edges_ref, 0, 0, devices)
    right = panel(edges_ref, 1, own_half() * (devices // 2), devices // 2)
    wide = dot(back_ref[:, : far_ref.shape[0]], far_ref[...]).astype(BF16)
    for h in range(share):
        k = slice(h * depth, (h + 1) * depth)
        here = [left[:, k], spread_ref[...]] + [ref[h] for ref in refs[:-1]]
        there = [right[:, k], wide[:, h * main : (h + 1) * main]]
        if len(refs) > 1:
            there.append(wide[:, share * main :])
        total = dot(jnp.concatenate(here, 1), jnp.concatenate(there, 1), NT).astype(BF16)
        for z in range(groups):
            out_ref[:, z, h] = total[:, z * cols : (z + 1) * cols].reshape(devices, rows, cols)


def last_kernel(*refs):
    gate_ref, gain_ref, bias_ref, weight_ref = refs[:4]
    out_ref = refs[-1]
    rows, cols = gate_ref.shape[:2]
    hidden = weight_ref.shape[0]
    parts = []
    for ref in refs[4:-1]:
        parts.append(ref[...].reshape(ref.shape[0] * ref.shape[1], rows, cols))
    value = jnp.swapaxes(jnp.concatenate(parts, 0), 0, 1)
    weight = weight_ref[...]
    gain = jnp.broadcast_to(gain_ref[...], (cols, hidden)).T
    bias = jnp.broadcast_to(bias_ref[...], (cols, hidden)).T
    for i in range(rows):
        product = value[i].astype(F32)
        average = jnp.mean(product, axis=0, keepdims=True)
        centered = product - average
        variance = jnp.mean(centered * centered, axis=0, keepdims=True)
        normed = centered * lax.rsqrt(variance + EPS) * gain + bias
        update = dot(normed.astype(BF16), weight, (((0,), (0,)), ((), ())))
        out_ref[i] = (gate_ref[i] * update).astype(BF16)


def shards(
    pair_rep,
    token_mask,
    in_gain,
    in_bias,
    left_weight,
    right_weight,
    gate_weight,
    out_gain,
    out_bias,
    out_weight,
):
    rows, cols, pair_width = pair_rep.shape
    hidden = out_weight.shape[0]
    row_count = lax.axis_size("row")
    col_count = lax.axis_size("col")
    group_cols = col_count // 2
    members = row_count * group_cols
    share = hidden // members
    chunks = CHUNKS if share % CHUNKS == 0 else 1
    share //= chunks
    width = hidden // chunks
    tokens = row_count * rows
    near_tokens = group_cols * cols
    axes = ("row", "col")
    groups = [
        [r * col_count + h * group_cols + z for r in range(row_count) for z in range(group_cols)]
        for h in range(2)
    ]
    across = [(c, (c + group_cols) % col_count) for c in range(col_count)]

    tile = min(ROW_TILE, rows)
    steps = rows // tile
    by_row = lambda *tail: pl.BlockSpec((tile,) + tail, lambda i: (i,) + (0,) * len(tail))
    edge_shape = jax.ShapeDtypeStruct((members, 2, share, rows, cols), BF16)
    edge_spec = pl.BlockSpec((members, 2, share, tile, cols), lambda i: (0, 0, 0, i, 0))
    mask_row = token_mask[None]
    mask_specs = [pl.BlockSpec(memory_space=pltpu.SMEM), whole(mask_row)]
    weight_specs = [whole(left_weight), whole(right_weight)]
    operands = (token_mask, mask_row, pair_rep, left_weight, right_weight)
    operands += (in_gain[None], in_bias[None])
    operand_specs = (
        mask_specs
        + [by_row(cols, pair_width)]
        + weight_specs
        + [whole(in_gain[None]), whole(in_bias[None])]
    )
    first, number = pl.pallas_call(
        functools.partial(first_kernel, width=width),
        grid=(steps,),
        in_specs=operand_specs,
        out_specs=[edge_spec, pl.BlockSpec(memory_space=pltpu.SMEM)],
        out_shape=[edge_shape, jax.ShapeDtypeStruct((1,), jnp.int32)],
        compiler_params=PARAMS,
        name="norm_project",
    )(*operands)

    def after(value, others):
        return lax.optimization_barrier((value, *others))[0] if others else value

    def exchange(value):
        return lax.all_to_all(value, axes, 0, 0, axis_index_groups=groups, tiled=True)

    main = tokens * 3 // 4
    pack = pack_of(share, tokens // 16)
    most = max(units for _, units in SIZES)
    all_pick, pick, back_pick, spread, *spreads = pl.pallas_call(
        picks_kernel,
        out_shape=[
            jax.ShapeDtypeStruct((tokens, tokens), BF16),
            jax.ShapeDtypeStruct((near_tokens, near_tokens), BF16),
            jax.ShapeDtypeStruct((near_tokens, near_tokens), BF16),
            jax.ShapeDtypeStruct((tokens, main), BF16),
        ]
        + [jax.ShapeDtypeStruct((share, tokens, pack), BF16)] * most,
        compiler_params=SMALL,
        cost_estimate=pl.CostEstimate(
            flops=64 * tokens * tokens, bytes_accessed=6 * tokens * tokens, transcendentals=0
        ),
        name="picks",
    )(mask_row)
    gate_shape = jax.ShapeDtypeStruct(pair_rep.shape, F32)
    gate, *edges = pl.pallas_call(
        functools.partial(gate_kernel, low=width, width=width * (chunks - 1)),
        grid=(steps,),
        in_specs=operand_specs + [whole(gate_weight)],
        out_specs=[by_row(cols, pair_width)] + [edge_spec] * (chunks - 1),
        out_shape=[gate_shape] + [edge_shape] * (chunks - 1),
        compiler_params=PARAMS,
        cost_estimate=pl.CostEstimate(
            flops=12 * rows * cols * pair_width * pair_width,
            bytes_accessed=10 * rows * cols * pair_width,
            transcendentals=3 * rows * cols * pair_width,
        ),
        name="gate_project",
    )(*operands[:2], after(pair_rep, [first, pick]), *operands[3:], gate_weight)
    arrived0 = exchange(first)
    arrived0, *edges = lax.optimization_barrier((arrived0, *edges))

    def middle(sizes, arrived0, edges, all_pick, pick, back_pick, spread, spreads):
        few, _, rest = counts(sizes, tokens)
        lanes = share * main + len(rest) * pack
        product_bytes = share * tokens * near_tokens * 6
        arrived = []
        sent = []
        fars = []
        for t in range(chunks):
            here = exchange(after(edges[t - 1], arrived[-1:])) if t else arrived0
            here = here.reshape(row_count, group_cols, 2, share, rows, cols)
            arrived.append(here)
            far = pl.pallas_call(
                functools.partial(far_kernel, main=main, rest=rest),
                out_shape=jax.ShapeDtypeStruct((few, lanes), BF16),
                compiler_params=SMALL,
                cost_estimate=pl.CostEstimate(
                    flops=6 * share * tokens * near_tokens * near_tokens,
                    bytes_accessed=product_bytes,
                    transcendentals=0,
                ),
                name="far_product",
            )(all_pick, pick, here)
            sent.append(far)
            fars.append(lax.ppermute(far, "col", across))
        back = []
        totals = []
        for t in range(chunks):
            total = pl.pallas_call(
                near_kernel,
                out_shape=jax.ShapeDtypeStruct((row_count, group_cols, share, rows, cols), BF16),
                compiler_params=SMALL,
                cost_estimate=pl.CostEstimate(
                    flops=NEAR_FLOPS, bytes_accessed=product_bytes, transcendentals=0
                ),
                name="near_product",
            )(
                back_pick,
                arrived[t],
                after(fars[t], sent[t + 1 : t + 2] + totals[-1:]),
                spread,
                *spreads[: len(rest)],
            )
            totals.append(total.reshape(members, share, rows, cols))
            if t < chunks - 1:
                back.append(exchange(totals[-1]))
        return *back, totals[-1]

    branches = [functools.partial(middle, sizes) for sizes in SIZES]
    *back, total = lax.switch(
        number[0], branches, arrived0, edges, all_pick, pick, back_pick, spread, spreads
    )
    back.append(exchange(total))
    piece = pl.BlockSpec((members, share, tile, cols), lambda i: (0, 0, i, 0))
    return pl.pallas_call(
        last_kernel,
        grid=(steps,),
        in_specs=[
            by_row(cols, pair_width),
            whole(out_gain[None]),
            whole(out_bias[None]),
            whole(out_weight),
        ]
        + [piece] * chunks,
        out_specs=by_row(cols, pair_width),
        out_shape=jax.ShapeDtypeStruct(pair_rep.shape, BF16),
        compiler_params=PARAMS,
        name="norm_out",
    )(gate, out_gain[None], out_bias[None], out_weight, *back)


def solution(mesh):
    placed = (P("row", "col", None), P(), P(), P(), P(), P(), P(), P(), P(), P())
    return jax.shard_map(
        shards, mesh=mesh, in_specs=placed, out_specs=P("row", "col", None), check_vma=False
    )
```

```python
import functools

import jax
import jax.numpy as jnp
from jax import lax
from jax.experimental import pallas as pl
from jax.experimental.pallas import tpu as pltpu
from jax.sharding import PartitionSpec as P

EPS = 1e-05
F32 = jnp.float32
BF16 = jnp.bfloat16
ROW_TILE = 32
CHUNKS = 2
NEAR_FLOPS = 2 * 10**10
PARAMS = pltpu.CompilerParams(vmem_limit_bytes=56 * 2**20)
SMALL = pltpu.CompilerParams(vmem_limit_bytes=24 * 2**20)
NT = (((1,), (1,)), ((), ()))
SIZES = ((12, 0), (13, 0), (13, 1), (14, 1), (14, 2), (15, 2), (16, 4))


def whole(array):
    return pl.BlockSpec(array.shape, lambda *_: (0,) * array.ndim)


def dot(left, right, dims=(((1,), (0,)), ((), ()))):
    return lax.dot_general(left, right, dims, preferred_element_type=F32)


def project(normed, tokens_ref, mask_ref, left_ref, right_ref, out_ref, low, width):
    rows, cols, pair_width = normed.shape
    hidden = left_ref.shape[1] // 2
    half = jnp.asarray(0.5, BF16)
    left = left_ref[...].T * half
    right = right_ref[...].T * half
    weight = jnp.concatenate(
        [
            left[low : low + width],
            right[low : low + width],
            left[hidden + low : hidden + low + width],
            right[hidden + low : hidden + low + width],
        ],
        0,
    )
    start = (lax.axis_index("row") * pl.num_programs(0) + pl.program_id(0)) * rows
    tokens = mask_ref.shape[1]
    valid = jnp.broadcast_to(mask_ref[...], (8, tokens)).astype(F32)
    valid = pltpu.roll(valid, lax.rem(tokens - lax.axis_index("col") * cols, tokens), 1)
    valid = valid[:1, :cols]
    pieces = []
    for i in range(0, rows, 2):
        two = normed[i : i + 2].reshape(2 * cols, pair_width)
        proj = dot(weight, two, NT)
        pair_valid = jnp.concatenate(
            [valid * tokens_ref[start + i + n].astype(F32) for n in range(2)], 1
        )
        value = (jnp.tanh(proj[: 2 * width]) + 1.0) * (proj[2 * width :] * pair_valid)
        value = value.astype(BF16)
        pieces += [value[:, :cols], value[:, cols:]]
    value = jnp.swapaxes(jnp.stack(pieces, 0), 0, 1)
    dests, _, share = out_ref.shape[:3]
    for side in range(2):
        part = value[side * width : (side + 1) * width]
        out_ref[:, side] = part.reshape(dests, share, rows, cols)


def normalise(pair_ref, gain_ref, bias_ref):
    rows, cols, pair_width = pair_ref.shape
    flat = pair_ref[...].reshape(rows * cols, pair_width)
    average = dot(flat, jnp.full((pair_width, pair_width), 1.0 / pair_width, BF16))
    centered = flat.astype(F32) - average
    variance = jnp.mean(centered * centered, axis=-1, keepdims=True)
    return (centered * lax.rsqrt(variance + EPS) * gain_ref[...] + bias_ref[...]).astype(BF16)


def first_kernel(
    tokens_ref, mask_ref, pair_ref, left_ref, right_ref, gain_ref, bias_ref, out_ref, number_ref, *, width
):
    normed = normalise(pair_ref, gain_ref, bias_ref).reshape(pair_ref.shape)
    project(normed, tokens_ref, mask_ref, left_ref, right_ref, out_ref, 0, width)
    size = mask_ref.shape[1] // 2
    low = jnp.sum(mask_ref[:, :size])
    high = jnp.sum(mask_ref[:, size:])
    number = len(SIZES) - 1
    for n in range(len(SIZES) - 2, -1, -1):
        few, main, rest = counts(SIZES[n], 2 * size)
        fits = (jnp.maximum(low, high) <= few) & (low + high <= main + sum(rest))
        number = jnp.where(fits, n, number)
    number_ref[0] = number


def gate_kernel(*refs, low, width):
    tokens_ref, mask_ref, pair_ref, left_ref, right_ref, gain_ref, bias_ref, weight_ref = refs[:8]
    flat = normalise(pair_ref, gain_ref, bias_ref)
    half = jnp.asarray(0.5, BF16)
    proj = dot(flat, weight_ref[...] * half)
    refs[8][...] = (0.5 * jnp.tanh(proj) + 0.5).reshape(pair_ref.shape)
    if width:
        normed = flat.reshape(pair_ref.shape)
        project(normed, tokens_ref, mask_ref, left_ref, right_ref, refs[9], low, width)


def counts(sizes, tokens):
    few, units = sizes
    return tokens // 2 * few // 16, tokens * 3 // 4, [tokens // 16] * units


def places(valid):
    size = valid.shape[1]
    above = lax.broadcasted_iota(jnp.int32, (size, size), 0)
    below = lax.broadcasted_iota(jnp.int32, (size, size), 1)
    through = dot(valid.astype(BF16), jnp.where(above <= below, 1.0, 0.0).astype(BF16))
    return jnp.where(valid > 0.5, through - 1.0, -1.0)[:1]


def ones_at(place, targets):
    return jnp.where(targets.astype(F32) == place, 1.0, 0.0)


def picks_kernel(tokens_ref, all_ref, pick_ref, back_ref, spread_ref, *rest_refs):
    tokens = tokens_ref.shape[1]
    valid = jnp.broadcast_to(tokens_ref[...].astype(F32), (16, tokens))
    place = places(valid)
    chosen = ones_at(place, lax.broadcasted_iota(jnp.int32, all_ref.shape, 0))
    all_ref[...] = chosen.astype(BF16)
    main = spread_ref.shape[1]
    spread_ref[...] = chosen[:main].T.astype(BF16)
    rest = (tokens - main) // len(rest_refs)
    for u, ref in enumerate(rest_refs):
        for h in range(ref.shape[0]):
            slot = lax.broadcasted_iota(jnp.int32, (ref.shape[2], tokens), 0) - h * rest
            target = jnp.where((slot >= 0) & (slot < rest), main + u * rest + slot, -2)
            ref[h] = ones_at(place, target).T.astype(BF16)
    size = tokens // 2
    low, high = places(valid[:, :size]), places(valid[:, size:])
    second = own_half() == 1
    order = lax.broadcasted_iota(jnp.int32, pick_ref.shape, 0)
    pick_ref[...] = ones_at(jnp.where(second, low, high), order).astype(BF16)
    back_ref[...] = ones_at(jnp.where(second, high, low), order).T.astype(BF16)


def pack_of(share, rest):
    return -(-share * rest // 128) * 128


def panel(ref, side, start, count):
    parts = []
    for h in range(ref.shape[3]):
        for z in range(ref.shape[1]):
            block = ref[pl.ds(start, count), z, side, h]
            parts.append(block.reshape(count * block.shape[1], block.shape[2]))
    return jnp.concatenate(parts, 1)


def own_half():
    return lax.axis_index("col") // (lax.axis_size("col") // 2)


def far_kernel(all_ref, pick_ref, edges_ref, far_ref, *, main, rest):
    devices, groups, _, share, rows, cols = edges_ref.shape
    depth = groups * cols
    left = panel(edges_ref, 0, 0, devices)
    right = panel(edges_ref, 1, (1 - own_half()) * (devices // 2), devices // 2)
    left = dot(all_ref[: main + sum(rest)], left).astype(BF16)
    right = dot(pick_ref[: far_ref.shape[0]], right).astype(BF16)
    for h in range(share):
        k = slice(h * depth, (h + 1) * depth)
        far_ref[:, h * main : (h + 1) * main] = dot(right[:, k], left[:main, k], NT).astype(BF16)
    at = share * main
    for u, size in enumerate(rest):
        few = left[main + u * size : main + (u + 1) * size]
        pack = pack_of(share, size)
        few = [few] * share
        if pack > share * size:
            few.append(jnp.zeros((pack - share * size, left.shape[1]), BF16))
        few = jnp.concatenate(few, 0)
        row_h = lax.broadcasted_iota(jnp.int32, few.shape, 0) // size
        lane_h = lax.broadcasted_iota(jnp.int32, few.shape, 1) // depth
        few = jnp.where(row_h == lane_h, few, jnp.zeros_like(few))
        far_ref[:, at : at + pack] = dot(right, few, NT).astype(BF16)
        at += pack


def near_kernel(back_ref, edges_ref, far_ref, spread_ref, *refs):
    out_ref = refs[-1]
    devices, groups, share, rows, cols = out_ref.shape
    depth = groups * cols
    main = spread_ref.shape[1]
    left = panel(edges_ref, 0, 0, devices)
    right = panel(edges_ref, 1, own_half() * (devices // 2), devices // 2)
    wide = dot(back_ref[:, : far_ref.shape[0]], far_ref[...]).astype(BF16)
    for h in range(share):
        k = slice(h * depth, (h + 1) * depth)
        here = [left[:, k], spread_ref[...]] + [ref[h] for ref in refs[:-1]]
        there = [right[:, k], wide[:, h * main : (h + 1) * main]]
        if len(refs) > 1:
            there.append(wide[:, share * main :])
        total = dot(jnp.concatenate(here, 1), jnp.concatenate(there, 1), NT).astype(BF16)
        for z in range(groups):
            out_ref[:, z, h] = total[:, z * cols : (z + 1) * cols].reshape(devices, rows, cols)


def last_kernel(*refs):
    gate_ref, gain_ref, bias_ref, weight_ref = refs[:4]
    out_ref = refs[-1]
    rows, cols = gate_ref.shape[:2]
    hidden = weight_ref.shape[0]
    parts = []
    for ref in refs[4:-1]:
        parts.append(ref[...].reshape(ref.shape[0] * ref.shape[1], rows, cols))
    value = jnp.swapaxes(jnp.concatenate(parts, 0), 0, 1)
    weight = weight_ref[...]
    gain = jnp.broadcast_to(gain_ref[...], (cols, hidden)).T
    bias = jnp.broadcast_to(bias_ref[...], (cols, hidden)).T
    for i in range(rows):
        product = value[i].astype(F32)
        average = jnp.mean(product, axis=0, keepdims=True)
        centered = product - average
        variance = jnp.mean(centered * centered, axis=0, keepdims=True)
        normed = centered * lax.rsqrt(variance + EPS) * gain + bias
        update = dot(normed.astype(BF16), weight, (((0,), (0,)), ((), ())))
        out_ref[i] = (gate_ref[i] * update).astype(BF16)


def shards(
    pair_rep,
    token_mask,
    in_gain,
    in_bias,
    left_weight,
    right_weight,
    gate_weight,
    out_gain,
    out_bias,
    out_weight,
):
    rows, cols, pair_width = pair_rep.shape
    hidden = out_weight.shape[0]
    row_count = lax.axis_size("row")
    col_count = lax.axis_size("col")
    group_cols = col_count // 2
    members = row_count * group_cols
    share = hidden // members
    chunks = CHUNKS if share % CHUNKS == 0 else 1
    share //= chunks
    width = hidden // chunks
    tokens = row_count * rows
    near_tokens = group_cols * cols
    axes = ("row", "col")
    groups = [
        [r * col_count + h * group_cols + z for r in range(row_count) for z in range(group_cols)]
        for h in range(2)
    ]
    across = [(c, (c + group_cols) % col_count) for c in range(col_count)]

    tile = min(ROW_TILE, rows)
    steps = rows // tile
    by_row = lambda *tail: pl.BlockSpec((tile,) + tail, lambda i: (i,) + (0,) * len(tail))
    edge_shape = jax.ShapeDtypeStruct((members, 2, share, rows, cols), BF16)
    edge_spec = pl.BlockSpec((members, 2, share, tile, cols), lambda i: (0, 0, 0, i, 0))
    mask_row = token_mask[None]
    mask_specs = [pl.BlockSpec(memory_space=pltpu.SMEM), whole(mask_row)]
    weight_specs = [whole(left_weight), whole(right_weight)]
    operands = (token_mask, mask_row, pair_rep, left_weight, right_weight)
    operands += (in_gain[None], in_bias[None])
    operand_specs = (
        mask_specs
        + [by_row(cols, pair_width)]
        + weight_specs
        + [whole(in_gain[None]), whole(in_bias[None])]
    )
    first, number = pl.pallas_call(
        functools.partial(first_kernel, width=width),
        grid=(steps,),
        in_specs=operand_specs,
        out_specs=[edge_spec, pl.BlockSpec(memory_space=pltpu.SMEM)],
        out_shape=[edge_shape, jax.ShapeDtypeStruct((1,), jnp.int32)],
        compiler_params=PARAMS,
        name="norm_project",
    )(*operands)

    def after(value, others):
        return lax.optimization_barrier((value, *others))[0] if others else value

    def exchange(value):
        return lax.all_to_all(value, axes, 0, 0, axis_index_groups=groups, tiled=True)

    main = tokens * 3 // 4
    pack = pack_of(share, tokens // 16)
    most = max(units for _, units in SIZES)
    all_pick, pick, back_pick, spread, *spreads = pl.pallas_call(
        picks_kernel,
        out_shape=[
            jax.ShapeDtypeStruct((tokens, tokens), BF16),
            jax.ShapeDtypeStruct((near_tokens, near_tokens), BF16),
            jax.ShapeDtypeStruct((near_tokens, near_tokens), BF16),
            jax.ShapeDtypeStruct((tokens, main), BF16),
        ]
        + [jax.ShapeDtypeStruct((share, tokens, pack), BF16)] * most,
        compiler_params=SMALL,
        cost_estimate=pl.CostEstimate(
            flops=64 * tokens * tokens, bytes_accessed=6 * tokens * tokens, transcendentals=0
        ),
        name="picks",
    )(mask_row)
    gate_shape = jax.ShapeDtypeStruct(pair_rep.shape, F32)
    gate, *edges = pl.pallas_call(
        functools.partial(gate_kernel, low=width, width=width * (chunks - 1)),
        grid=(steps,),
        in_specs=operand_specs + [whole(gate_weight)],
        out_specs=[by_row(cols, pair_width)] + [edge_spec] * (chunks - 1),
        out_shape=[gate_shape] + [edge_shape] * (chunks - 1),
        compiler_params=PARAMS,
        cost_estimate=pl.CostEstimate(
            flops=12 * rows * cols * pair_width * pair_width,
            bytes_accessed=10 * rows * cols * pair_width,
            transcendentals=3 * rows * cols * pair_width,
        ),
        name="gate_project",
    )(*operands[:2], after(pair_rep, [first, pick]), *operands[3:], gate_weight)
    arrived0 = exchange(first)
    arrived0, *edges = lax.optimization_barrier((arrived0, *edges))

    def middle(sizes, arrived0, edges, all_pick, pick, back_pick, spread, spreads):
        few, _, rest = counts(sizes, tokens)
        lanes = share * main + len(rest) * pack
        product_bytes = share * tokens * near_tokens * 6
        arrived = []
        sent = []
        fars = []
        for t in range(chunks):
            here = exchange(after(edges[t - 1], arrived[-1:])) if t else arrived0
            here = here.reshape(row_count, group_cols, 2, share, rows, cols)
            arrived.append(here)
            far = pl.pallas_call(
                functools.partial(far_kernel, main=main, rest=rest),
                out_shape=jax.ShapeDtypeStruct((few, lanes), BF16),
                compiler_params=SMALL,
                cost_estimate=pl.CostEstimate(
                    flops=6 * share * tokens * near_tokens * near_tokens,
                    bytes_accessed=product_bytes,
                    transcendentals=0,
                ),
                name="far_product",
            )(all_pick, pick, here)
            sent.append(far)
            fars.append(lax.ppermute(far, "col", across))
        back = []
        totals = []
        for t in range(chunks):
            total = pl.pallas_call(
                near_kernel,
                out_shape=jax.ShapeDtypeStruct((row_count, group_cols, share, rows, cols), BF16),
                compiler_params=SMALL,
                cost_estimate=pl.CostEstimate(
                    flops=NEAR_FLOPS, bytes_accessed=product_bytes, transcendentals=0
                ),
                name="near_product",
            )(
                back_pick,
                arrived[t],
                after(fars[t], sent[t + 1 : t + 2] + totals[-1:]),
                spread,
                *spreads[: len(rest)],
            )
            totals.append(total.reshape(members, share, rows, cols))
            if t < chunks - 1:
                back.append(exchange(totals[-1]))
        return *back, totals[-1]

    branches = [functools.partial(middle, sizes) for sizes in SIZES]
    *back, total = lax.switch(
        number[0], branches, arrived0, edges, all_pick, pick, back_pick, spread, spreads
    )
    back.append(exchange(total))
    piece = pl.BlockSpec((members, share, tile, cols), lambda i: (0, 0, i, 0))
    return pl.pallas_call(
        last_kernel,
        grid=(steps,),
        in_specs=[
            by_row(cols, pair_width),
            whole(out_gain[None]),
            whole(out_bias[None]),
            whole(out_weight),
        ]
        + [piece] * chunks,
        out_specs=by_row(cols, pair_width),
        out_shape=jax.ShapeDtypeStruct(pair_rep.shape, BF16),
        compiler_params=PARAMS,
        name="norm_out",
    )(gate, out_gain[None], out_bias[None], out_weight, *back)


def solution(mesh):
    placed = (P("row", "col", None), P(), P(), P(), P(), P(), P(), P(), P(), P())
    return jax.shard_map(
        shards, mesh=mesh, in_specs=placed, out_specs=P("row", "col", None), check_vma=False
    )
```

```python
import functools

import jax
import jax.numpy as jnp
from jax import lax
from jax.experimental import pallas as pl
from jax.experimental.pallas import tpu as pltpu
from jax.sharding import PartitionSpec as P

EPS = 1e-05
F32 = jnp.float32
BF16 = jnp.bfloat16
ROW_TILE = 32
CHUNKS = 2
NEAR_FLOPS = 2 * 10**10
PARAMS = pltpu.CompilerParams(vmem_limit_bytes=56 * 2**20)
SMALL = pltpu.CompilerParams(vmem_limit_bytes=24 * 2**20)
NT = (((1,), (1,)), ((), ()))
SIZES = ((12, 0), (13, 0), (13, 1), (14, 1), (14, 2), (15, 2), (16, 4))


def whole(array):
    return pl.BlockSpec(array.shape, lambda *_: (0,) * array.ndim)


def dot(left, right, dims=(((1,), (0,)), ((), ()))):
    return lax.dot_general(left, right, dims, preferred_element_type=F32)


def project(normed, tokens_ref, mask_ref, left_ref, right_ref, out_ref, low, width):
    rows, cols, pair_width = normed.shape
    hidden = left_ref.shape[1] // 2
    half = jnp.asarray(0.5, BF16)
    left = left_ref[...].T * half
    right = right_ref[...].T * half
    weight = jnp.concatenate(
        [
            left[low : low + width],
            right[low : low + width],
            left[hidden + low : hidden + low + width],
            right[hidden + low : hidden + low + width],
        ],
        0,
    )
    start = (lax.axis_index("row") * pl.num_programs(0) + pl.program_id(0)) * rows
    tokens = mask_ref.shape[1]
    valid = jnp.broadcast_to(mask_ref[...], (8, tokens)).astype(F32)
    valid = pltpu.roll(valid, lax.rem(tokens - lax.axis_index("col") * cols, tokens), 1)
    valid = valid[:1, :cols]
    pieces = []
    for i in range(0, rows, 2):
        two = normed[i : i + 2].reshape(2 * cols, pair_width)
        proj = dot(weight, two, NT)
        pair_valid = jnp.concatenate(
            [valid * tokens_ref[start + i + n].astype(F32) for n in range(2)], 1
        )
        value = (jnp.tanh(proj[: 2 * width]) + 1.0) * (proj[2 * width :] * pair_valid)
        value = value.astype(BF16)
        pieces += [value[:, :cols], value[:, cols:]]
    value = jnp.swapaxes(jnp.stack(pieces, 0), 0, 1)
    dests, _, share = out_ref.shape[:3]
    for side in range(2):
        part = value[side * width : (side + 1) * width]
        out_ref[:, side] = part.reshape(dests, share, rows, cols)


def normalise(pair_ref, gain_ref, bias_ref):
    rows, cols, pair_width = pair_ref.shape
    flat = pair_ref[...].reshape(rows * cols, pair_width)
    average = dot(flat, jnp.full((pair_width, pair_width), 1.0 / pair_width, BF16))
    centered = flat.astype(F32) - average
    variance = jnp.mean(centered * centered, axis=-1, keepdims=True)
    return (centered * lax.rsqrt(variance + EPS) * gain_ref[...] + bias_ref[...]).astype(BF16)


def first_kernel(
    tokens_ref, mask_ref, pair_ref, left_ref, right_ref, gain_ref, bias_ref, out_ref, number_ref, *, width
):
    normed = normalise(pair_ref, gain_ref, bias_ref).reshape(pair_ref.shape)
    project(normed, tokens_ref, mask_ref, left_ref, right_ref, out_ref, 0, width)
    size = mask_ref.shape[1] // 2
    low = jnp.sum(mask_ref[:, :size])
    high = jnp.sum(mask_ref[:, size:])
    number = len(SIZES) - 1
    for n in range(len(SIZES) - 2, -1, -1):
        few, main, rest = counts(SIZES[n], 2 * size)
        fits = (jnp.maximum(low, high) <= few) & (low + high <= main + sum(rest))
        number = jnp.where(fits, n, number)
    number_ref[0] = number


def gate_kernel(*refs, low, width):
    tokens_ref, mask_ref, pair_ref, left_ref, right_ref, gain_ref, bias_ref, weight_ref = refs[:8]
    flat = normalise(pair_ref, gain_ref, bias_ref)
    half = jnp.asarray(0.5, BF16)
    proj = dot(flat, weight_ref[...] * half)
    refs[8][...] = (0.5 * jnp.tanh(proj) + 0.5).reshape(pair_ref.shape)
    if width:
        normed = flat.reshape(pair_ref.shape)
        project(normed, tokens_ref, mask_ref, left_ref, right_ref, refs[9], low, width)


def counts(sizes, tokens):
    few, units = sizes
    return tokens // 2 * few // 16, tokens * 3 // 4, [tokens // 16] * units


def places(valid):
    size = valid.shape[1]
    above = lax.broadcasted_iota(jnp.int32, (size, size), 0)
    below = lax.broadcasted_iota(jnp.int32, (size, size), 1)
    through = dot(valid.astype(BF16), jnp.where(above <= below, 1.0, 0.0).astype(BF16))
    return jnp.where(valid > 0.5, through - 1.0, -1.0)[:1]


def ones_at(place, targets):
    return jnp.where(targets.astype(F32) == place, 1.0, 0.0)


def picks_kernel(tokens_ref, all_ref, pick_ref, back_ref, spread_ref, *rest_refs):
    tokens = tokens_ref.shape[1]
    valid = jnp.broadcast_to(tokens_ref[...].astype(F32), (16, tokens))
    place = places(valid)
    chosen = ones_at(place, lax.broadcasted_iota(jnp.int32, all_ref.shape, 0))
    all_ref[...] = chosen.astype(BF16)
    main = spread_ref.shape[1]
    spread_ref[...] = chosen[:main].T.astype(BF16)
    rest = (tokens - main) // len(rest_refs)
    for u, ref in enumerate(rest_refs):
        for h in range(ref.shape[0]):
            slot = lax.broadcasted_iota(jnp.int32, (ref.shape[2], tokens), 0) - h * rest
            target = jnp.where((slot >= 0) & (slot < rest), main + u * rest + slot, -2)
            ref[h] = ones_at(place, target).T.astype(BF16)
    size = tokens // 2
    low, high = places(valid[:, :size]), places(valid[:, size:])
    second = own_half() == 1
    order = lax.broadcasted_iota(jnp.int32, pick_ref.shape, 0)
    pick_ref[...] = ones_at(jnp.where(second, low, high), order).astype(BF16)
    back_ref[...] = ones_at(jnp.where(second, high, low), order).T.astype(BF16)


def pack_of(share, rest):
    return -(-share * rest // 128) * 128


def panel(ref, side, start, count):
    parts = []
    for h in range(ref.shape[3]):
        for z in range(ref.shape[1]):
            block = ref[pl.ds(start, count), z, side, h]
            parts.append(block.reshape(count * block.shape[1], block.shape[2]))
    return jnp.concatenate(parts, 1)


def own_half():
    return lax.axis_index("col") // (lax.axis_size("col") // 2)


def far_kernel(all_ref, pick_ref, edges_ref, far_ref, *, main, rest):
    devices, groups, _, share, rows, cols = edges_ref.shape
    depth = groups * cols
    left = panel(edges_ref, 0, 0, devices)
    right = panel(edges_ref, 1, (1 - own_half()) * (devices // 2), devices // 2)
    left = dot(all_ref[: main + sum(rest)], left).astype(BF16)
    right = dot(pick_ref[: far_ref.shape[0]], right).astype(BF16)
    for h in range(share):
        k = slice(h * depth, (h + 1) * depth)
        far_ref[:, h * main : (h + 1) * main] = dot(right[:, k], left[:main, k], NT).astype(BF16)
    at = share * main
    for u, size in enumerate(rest):
        few = left[main + u * size : main + (u + 1) * size]
        pack = pack_of(share, size)
        few = [few] * share
        if pack > share * size:
            few.append(jnp.zeros((pack - share * size, left.shape[1]), BF16))
        few = jnp.concatenate(few, 0)
        row_h = lax.broadcasted_iota(jnp.int32, few.shape, 0) // size
        lane_h = lax.broadcasted_iota(jnp.int32, few.shape, 1) // depth
        few = jnp.where(row_h == lane_h, few, jnp.zeros_like(few))
        far_ref[:, at : at + pack] = dot(right, few, NT).astype(BF16)
        at += pack


def near_kernel(back_ref, edges_ref, far_ref, spread_ref, *refs):
    out_ref = refs[-1]
    devices, groups, share, rows, cols = out_ref.shape
    depth = groups * cols
    main = spread_ref.shape[1]
    left = panel(edges_ref, 0, 0, devices)
    right = panel(edges_ref, 1, own_half() * (devices // 2), devices // 2)
    wide = dot(back_ref[:, : far_ref.shape[0]], far_ref[...]).astype(BF16)
    for h in range(share):
        k = slice(h * depth, (h + 1) * depth)
        here = [left[:, k], spread_ref[...]] + [ref[h] for ref in refs[:-1]]
        there = [right[:, k], wide[:, h * main : (h + 1) * main]]
        if len(refs) > 1:
            there.append(wide[:, share * main :])
        total = dot(jnp.concatenate(here, 1), jnp.concatenate(there, 1), NT).astype(BF16)
        for z in range(groups):
            out_ref[:, z, h] = total[:, z * cols : (z + 1) * cols].reshape(devices, rows, cols)


def last_kernel(*refs):
    gate_ref, gain_ref, bias_ref, weight_ref = refs[:4]
    out_ref = refs[-1]
    rows, cols = gate_ref.shape[:2]
    hidden = weight_ref.shape[0]
    parts = []
    for ref in refs[4:-1]:
        parts.append(ref[...].reshape(ref.shape[0] * ref.shape[1], rows, cols))
    value = jnp.concatenate(parts, 0)
    weight = weight_ref[...]
    gain = jnp.broadcast_to(gain_ref[...], (cols, hidden)).T[:, None, :]
    bias = jnp.broadcast_to(bias_ref[...], (cols, hidden)).T[:, None, :]
    some = min(16, rows)
    for start in range(0, rows, some):
        product = value[:, start : start + some].astype(F32)
        average = jnp.mean(product, axis=0, keepdims=True)
        centered = product - average
        variance = jnp.mean(centered * centered, axis=0, keepdims=True)
        normed = centered * lax.rsqrt(variance + EPS) * gain + bias
        normed = jnp.swapaxes(normed.astype(BF16), 0, 1)
        for i in range(some):
            update = dot(normed[i], weight, (((0,), (0,)), ((), ())))
            out_ref[start + i] = (gate_ref[start + i] * update).astype(BF16)


def shards(
    pair_rep,
    token_mask,
    in_gain,
    in_bias,
    left_weight,
    right_weight,
    gate_weight,
    out_gain,
    out_bias,
    out_weight,
):
    rows, cols, pair_width = pair_rep.shape
    hidden = out_weight.shape[0]
    row_count = lax.axis_size("row")
    col_count = lax.axis_size("col")
    group_cols = col_count // 2
    members = row_count * group_cols
    share = hidden // members
    chunks = CHUNKS if share % CHUNKS == 0 else 1
    share //= chunks
    width = hidden // chunks
    tokens = row_count * rows
    near_tokens = group_cols * cols
    axes = ("row", "col")
    groups = [
        [r * col_count + h * group_cols + z for r in range(row_count) for z in range(group_cols)]
        for h in range(2)
    ]
    across = [(c, (c + group_cols) % col_count) for c in range(col_count)]

    tile = min(ROW_TILE, rows)
    steps = rows // tile
    by_row = lambda *tail: pl.BlockSpec((tile,) + tail, lambda i: (i,) + (0,) * len(tail))
    edge_shape = jax.ShapeDtypeStruct((members, 2, share, rows, cols), BF16)
    edge_spec = pl.BlockSpec((members, 2, share, tile, cols), lambda i: (0, 0, 0, i, 0))
    mask_row = token_mask[None]
    mask_specs = [pl.BlockSpec(memory_space=pltpu.SMEM), whole(mask_row)]
    weight_specs = [whole(left_weight), whole(right_weight)]
    operands = (token_mask, mask_row, pair_rep, left_weight, right_weight)
    operands += (in_gain[None], in_bias[None])
    operand_specs = (
        mask_specs
        + [by_row(cols, pair_width)]
        + weight_specs
        + [whole(in_gain[None]), whole(in_bias[None])]
    )
    first, number = pl.pallas_call(
        functools.partial(first_kernel, width=width),
        grid=(steps,),
        in_specs=operand_specs,
        out_specs=[edge_spec, pl.BlockSpec(memory_space=pltpu.SMEM)],
        out_shape=[edge_shape, jax.ShapeDtypeStruct((1,), jnp.int32)],
        compiler_params=PARAMS,
        name="norm_project",
    )(*operands)

    def after(value, others):
        return lax.optimization_barrier((value, *others))[0] if others else value

    def exchange(value):
        return lax.all_to_all(value, axes, 0, 0, axis_index_groups=groups, tiled=True)

    main = tokens * 3 // 4
    pack = pack_of(share, tokens // 16)
    most = max(units for _, units in SIZES)
    all_pick, pick, back_pick, spread, *spreads = pl.pallas_call(
        picks_kernel,
        out_shape=[
            jax.ShapeDtypeStruct((tokens, tokens), BF16),
            jax.ShapeDtypeStruct((near_tokens, near_tokens), BF16),
            jax.ShapeDtypeStruct((near_tokens, near_tokens), BF16),
            jax.ShapeDtypeStruct((tokens, main), BF16),
        ]
        + [jax.ShapeDtypeStruct((share, tokens, pack), BF16)] * most,
        compiler_params=SMALL,
        cost_estimate=pl.CostEstimate(
            flops=64 * tokens * tokens, bytes_accessed=6 * tokens * tokens, transcendentals=0
        ),
        name="picks",
    )(mask_row)
    gate_shape = jax.ShapeDtypeStruct(pair_rep.shape, F32)
    gate, *edges = pl.pallas_call(
        functools.partial(gate_kernel, low=width, width=width * (chunks - 1)),
        grid=(steps,),
        in_specs=operand_specs + [whole(gate_weight)],
        out_specs=[by_row(cols, pair_width)] + [edge_spec] * (chunks - 1),
        out_shape=[gate_shape] + [edge_shape] * (chunks - 1),
        compiler_params=PARAMS,
        cost_estimate=pl.CostEstimate(
            flops=12 * rows * cols * pair_width * pair_width,
            bytes_accessed=10 * rows * cols * pair_width,
            transcendentals=3 * rows * cols * pair_width,
        ),
        name="gate_project",
    )(*operands[:2], after(pair_rep, [first, pick]), *operands[3:], gate_weight)
    arrived0 = exchange(first)
    arrived0, *edges = lax.optimization_barrier((arrived0, *edges))

    def middle(sizes, arrived0, edges, all_pick, pick, back_pick, spread, spreads):
        few, _, rest = counts(sizes, tokens)
        lanes = share * main + len(rest) * pack
        product_bytes = share * tokens * near_tokens * 6
        arrived = []
        sent = []
        fars = []
        for t in range(chunks):
            here = exchange(after(edges[t - 1], arrived[-1:])) if t else arrived0
            here = here.reshape(row_count, group_cols, 2, share, rows, cols)
            arrived.append(here)
            far = pl.pallas_call(
                functools.partial(far_kernel, main=main, rest=rest),
                out_shape=jax.ShapeDtypeStruct((few, lanes), BF16),
                compiler_params=SMALL,
                cost_estimate=pl.CostEstimate(
                    flops=6 * share * tokens * near_tokens * near_tokens,
                    bytes_accessed=product_bytes,
                    transcendentals=0,
                ),
                name="far_product",
            )(all_pick, pick, here)
            sent.append(far)
            fars.append(lax.ppermute(far, "col", across))
        back = []
        totals = []
        for t in range(chunks):
            total = pl.pallas_call(
                near_kernel,
                out_shape=jax.ShapeDtypeStruct((row_count, group_cols, share, rows, cols), BF16),
                compiler_params=SMALL,
                cost_estimate=pl.CostEstimate(
                    flops=NEAR_FLOPS, bytes_accessed=product_bytes, transcendentals=0
                ),
                name="near_product",
            )(
                back_pick,
                arrived[t],
                after(fars[t], sent[t + 1 : t + 2] + totals[-1:]),
                spread,
                *spreads[: len(rest)],
            )
            totals.append(total.reshape(members, share, rows, cols))
            if t < chunks - 1:
                back.append(exchange(totals[-1]))
        return *back, totals[-1]

    branches = [functools.partial(middle, sizes) for sizes in SIZES]
    *back, total = lax.switch(
        number[0], branches, arrived0, edges, all_pick, pick, back_pick, spread, spreads
    )
    back.append(exchange(total))
    piece = pl.BlockSpec((members, share, tile, cols), lambda i: (0, 0, i, 0))
    return pl.pallas_call(
        last_kernel,
        grid=(steps,),
        in_specs=[
            by_row(cols, pair_width),
            whole(out_gain[None]),
            whole(out_bias[None]),
            whole(out_weight),
        ]
        + [piece] * chunks,
        out_specs=by_row(cols, pair_width),
        out_shape=jax.ShapeDtypeStruct(pair_rep.shape, BF16),
        compiler_params=PARAMS,
        name="norm_out",
    )(gate, out_gain[None], out_bias[None], out_weight, *back)


def solution(mesh):
    placed = (P("row", "col", None), P(), P(), P(), P(), P(), P(), P(), P(), P())
    return jax.shard_map(
        shards, mesh=mesh, in_specs=placed, out_specs=P("row", "col", None), check_vma=False
    )
```
